128 devices in a mesh: tile: 16 (over y_hi, z, core), hid: 8 (over x, y_lo).
Axes of the slice: x: 4, y: 4 (y_hi: 2, y_lo: 2; y = y_hi * 2 + y_lo), z: 4, core: 2. Of those that a mesh axis runs over, the one named last changes fastest.
Arguments:
- residual_in: bfloat16 [8192, 6144], P('tile', 'hid'), may hold values from -68 to 68
- w_query: bfloat16 [6144, 3072], P('tile', 'hid'), may hold values from -0.078125 to 0.078125
- w_key: bfloat16 [6144, 3072], P('tile', 'hid'), may hold values from -0.078125 to 0.078125
- w_value: bfloat16 [6144, 3072], P('tile', 'hid'), may hold values from -0.078125 to 0.078125
- w_output: bfloat16 [3072, 6144], P('hid', 'tile'), may hold values from -0.109375 to 0.109375
- shift_mod: float32 [6144], replicated, may hold values from -4 to 4
- scale_mod: float32 [6144], replicated, may hold values from 0.5 to 11
- gate_mod: float32 [6144], replicated, may hold values from 0.5 to 1.5
- neighbours: int32 [256, 27], P('tile'), may hold values from -1 to 255, as said below
Outputs:
- block_out: bfloat16 [8192, 6144], P('tile', 'hid')
The draws below stay inside these ranges and needn't reach their ends.
Inputs may be any that keep to these rules, and one draw needn't show every extreme that they name: `neighbours`: entry j of a tile's row is either -1 or the number of the tile at offset j; it is -1 where that tile lies outside the grid of 16 x 4 x 4 tiles (tile layers x tile rows x tile columns); the entry of offset 13 (the tile itself) is never -1.
All inputs are finite; a program needn't handle non-finite values.
Results may differ from the reference program's by a relative error of at most 0.02.
The reference program's roundings to bfloat16 on the way (of `modded`, `queries`, `soft` and `attended`) count: a program that leaves them out, or rounds other values in their place, can miss the bound.
Values may be sent and summed in bfloat16 or wider, within the bound.
No kernel may reach another device: no remote copies, remote signals or barrier semaphores. Data moves between devices by JAX's collectives and lax.ppermute only.
A program may use at most 128 MiB of HBM per device.

```python
import math
import jax
import jax.numpy as jnp
from jax import lax

D = 6144
HEADS = 24
HD = 128
TT = 2
TH = 4
TW = 4
HH = 16
WW = 16
NBR = 27
FRAMES = 32
TOKENS = 8192
TILES = 256


def draw_residual_in(key, part):
    key = jax.random.fold_in(key, 11)
    key_base, key_rows, key_cols = jax.random.split(key, 3)
    positions = jnp.arange(D, dtype=jnp.float32) / D
    ramp_up = 0.3 * jnp.exp(positions * math.log(10.0))[None, :]
    row_scale = jnp.exp(jax.random.uniform(key_rows, (TOKENS, 1), jnp.float32, math.log(0.3), math.log(3.0)))
    jitter = jnp.exp(jax.random.uniform(key_cols, (1, D), jnp.float32, math.log(0.8), math.log(1.25)))
    base = jnp.clip(jax.random.normal(key_base, (TOKENS, D), jnp.float32), -6.0, 6.0)
    return (base * row_scale * ramp_up * jitter).astype(jnp.bfloat16)


def draw_scale_mod(key, part):
    key = jax.random.fold_in(key, 23)
    return jax.random.uniform(key, (D,), jnp.float32, 0.5, 1.5)


def draw_neighbours(key, part):
    key = jax.random.fold_in(key, 37)
    per_row = HH // TH
    per_col = WW // TW
    per_layer = per_row * per_col
    layer_total = FRAMES // TT
    tile_ids = jnp.arange(TILES, dtype=jnp.int32)
    layer_of = tile_ids // per_layer
    row_of = tile_ids % per_layer // per_col
    col_of = tile_ids % per_col
    offset_ids = jnp.arange(NBR, dtype=jnp.int32)
    step_layer = offset_ids // 9 - 1
    step_row = offset_ids // 3 % 3 - 1
    step_col = offset_ids % 3 - 1
    new_layer = layer_of[:, None] + step_layer[None, :]
    new_row = row_of[:, None] + step_row[None, :]
    new_col = col_of[:, None] + step_col[None, :]
    inside = (new_layer >= 0) & (new_layer < layer_total) & (new_row >= 0) & (new_row < per_row) & (new_col >= 0) & (new_col < per_col)
    target = new_layer * per_layer + new_row * per_col + new_col
    retained = jax.random.randint(key, (TILES, NBR), 0, 4) != 0
    retained = retained | (offset_ids == 13)[None, :]
    return jnp.where(inside & retained, target, -1).astype(jnp.int32)


def level_of(key, shape, cuts, least, top_value):
    gain, own = 1.0, jax.random.fold_in(key, 6)
    for position, blocks in cuts:
        draws = jnp.exp(jax.random.uniform(jax.random.fold_in(own, position), (blocks,), jnp.float32, least / len(cuts), top_value / len(cuts)))
        gain = gain * jnp.repeat(draws, shape[position] // blocks).reshape([-1 if axis == position else 1 for axis in range(len(shape))])
    return gain


def centred(rng, dims, scale, limit, shards=(), kind=jnp.bfloat16):
    gain = level_of(rng, dims, shards, -0.22, 0.18) if shards else 1.0
    entries = jax.random.normal(rng, dims, jnp.float32) * scale * gain
    return jnp.minimum(jnp.maximum(entries, -limit), limit).astype(kind)


def setup_inputs(seed: int = 0) -> dict:
    splits = jax.random.split(jax.random.key(seed), 10)
    residual_in = draw_residual_in(jax.random.fold_in(splits[9], 71), 0)
    w_query = centred(splits[1], (D, HEADS * HD), D ** -0.5, 0.078125, ((0, 16), (1, 8)))
    w_key = centred(splits[2], (D, HEADS * HD), D ** -0.5, 0.078125, ((0, 16), (1, 8)))
    w_value = centred(splits[3], (D, HEADS * HD), D ** -0.5, 0.078125, ((0, 16), (1, 8)))
    w_output = centred(splits[4], (HEADS * HD, D), (HEADS * HD) ** -0.5, 0.109375, ((0, 8), (1, 16)))
    shift_mod = centred(splits[5], (D,), 1.0, 4.0, (), jnp.float32)
    scale_mod = draw_scale_mod(jax.random.fold_in(splits[9], 71), 0)
    gate_mod = jnp.clip(jax.random.uniform(splits[7], (D,), jnp.float32, 0.5, 1.5), 0.5, 1.5)
    neighbours = draw_neighbours(jax.random.fold_in(splits[9], 71), 0)
    return {"residual_in": residual_in, "w_query": w_query, "w_key": w_key, "w_value": w_value, "w_output": w_output, "shift_mod": shift_mod, "scale_mod": scale_mod, "gate_mod": gate_mod, "neighbours": neighbours}


def reference(residual_in, w_query, w_key, w_value, w_output, shift_mod, scale_mod, gate_mod, neighbours):
    stream = residual_in.astype(jnp.float32)
    centre = lax.optimization_barrier(jnp.mean(stream, axis=1, keepdims=True))
    spread = lax.optimization_barrier(jnp.mean((stream - centre) * (stream - centre), axis=1, keepdims=True))
    normed = (stream - centre) * lax.rsqrt(spread + 1e-06)
    modded = (normed * (1.0 + scale_mod) + shift_mod).astype(jnp.bfloat16)
    queries = jnp.dot(modded, w_query, preferred_element_type=jnp.float32).astype(jnp.bfloat16)
    key_rows = jnp.dot(modded, w_key, preferred_element_type=jnp.float32).astype(jnp.bfloat16)
    value_rows = jnp.dot(modded, w_value, preferred_element_type=jnp.float32).astype(jnp.bfloat16)
    tile_len = TT * TH * TW
    tile_count = queries.shape[0] // tile_len
    head_width = HEADS * HD
    query_tiles = queries.reshape(tile_count, tile_len, HEADS, HD)
    key_tiles = key_rows.reshape(tile_count, tile_len, HEADS, HD)
    value_tiles = value_rows.reshape(tile_count, tile_len, HEADS, HD)

    def one_tile(operands):
        query_tile, tile_ids = operands
        clipped = jnp.maximum(tile_ids, 0)
        near_keys = key_tiles[clipped].astype(jnp.float32)
        near_values = value_tiles[clipped].astype(jnp.float32)
        scores = jnp.einsum('qhd,jkhd->hqjk', query_tile.astype(jnp.float32), near_keys) * HD ** (-0.5)
        listed = (tile_ids >= 0)[None, None, :, None]
        scores = jnp.where(listed, scores, -1e+30)
        peak_val = lax.optimization_barrier(jnp.max(scores, axis=(2, 3), keepdims=True))
        chance = jnp.exp(scores - peak_val)
        denom_sum = lax.optimization_barrier(jnp.sum(chance, axis=(2, 3)))
        soft = chance.astype(jnp.bfloat16).astype(jnp.float32)
        blended = jnp.einsum('hqjk,jkhd->qhd', soft, near_values)
        blended = blended / jnp.transpose(denom_sum)[:, :, None]
        return blended.astype(jnp.bfloat16).reshape(tile_len, head_width)
    attended = lax.map(one_tile, (query_tiles, neighbours)).reshape(-1, head_width)
    out_term = jnp.dot(attended, w_output, preferred_element_type=jnp.float32)
    return (stream + gate_mod * out_term).astype(jnp.bfloat16)
```

```python
import functools

import jax
import jax.numpy as jnp
import numpy as np
from jax import lax
from jax.experimental import pallas as pl
from jax.experimental.pallas import tpu as pltpu
from jax.sharding import PartitionSpec as P

HD = 128
TILE = 32
PER_ROW = 4
PER_LAYER = 16
LAYER = PER_LAYER * TILE
AXES = ("tile", "hid")
F32 = jnp.float32
BF16 = jnp.bfloat16


def route(move):
    pairs = []
    for x in range(4):
        for yl in range(2):
            for yh in range(2):
                for z in range(4):
                    for c in range(2):
                        a, b, d, e, f = move(x, yl, yh, z, c)
                        source = (yh * 8 + z * 2 + c) * 8 + x * 2 + yl
                        target = (d * 8 + e % 4 * 2 + f) * 8 + a % 4 * 2 + b
                        pairs.append((source, target))
    return pairs


def way(c):
    return 1 - 2 * c


X_A = route(lambda x, yl, yh, z, c: (x + way(c), yl, yh, z, c))
X_B = route(lambda x, yl, yh, z, c: (x - way(c), yl, yh, z, c))
X_1 = route(lambda x, yl, yh, z, c: (x ^ 1, yl, yh, z, c))
X_2 = route(lambda x, yl, yh, z, c: (x + 2, yl, yh, z, c))
Z_A = route(lambda x, yl, yh, z, c: (x, yl, yh, z + way(c), c))
Z_B = route(lambda x, yl, yh, z, c: (x, yl, yh, z - way(c), c))
Y_LO = route(lambda x, yl, yh, z, c: (x, 1 - yl, yh, z, c))
Y_HI = route(lambda x, yl, yh, z, c: (x, yl, 1 - yh, z, c))
CORE = route(lambda x, yl, yh, z, c: (x, yl, yh, z, 1 - c))
SWAP = route(lambda x, yl, yh, z, c: ((yh * 4 + z) // 2, z % 2, (x * 2 + yl) // 4, (x * 2 + yl) % 4, c))
NEXT = [(t * 8 + h, t * 8 + 8 + h) for t in range(15) for h in range(8)]
PREV = [(t * 8 + 8 + h, t * 8 + h) for t in range(15) for h in range(8)]


def send(array, pairs):
    return lax.ppermute(array, AXES, pairs)


def after(array, *others):
    return lax.optimization_barrier((array, *others))[0]


def start_weights(table, first, per, own, other, w_all, sems, depth):
    half = depth // 2
    for i in range(8):
        for part, refs_of in enumerate((own, other)):
            place = table[first[part] + i]
            target = w_all.at[pl.ds(i * depth + part * half, half), :]
            if len(refs_of) == 1:
                pltpu.make_async_copy(refs_of[0].at[place], target, sems.at[i]).start()
            else:

                @pl.when(place < per)
                def _():
                    source = refs_of[0].at[jnp.minimum(place, per - 1)]
                    pltpu.make_async_copy(source, target, sems.at[i]).start()

                @pl.when(place >= per)
                def _():
                    source = refs_of[1].at[jnp.maximum(place - per, 0)]
                    pltpu.make_async_copy(source, target, sems.at[i]).start()


def wait_weights(own, w_all, sems, depth, i):
    half = depth // 2
    for part in range(2):
        target = w_all.at[pl.ds(i * depth + part * half, half), :]
        pltpu.make_async_copy(own[0].at[0], target, sems.at[i]).wait()


PIECES = ((0, 1), (1, 2), (2, 4), (4, 6), (6, 8))
VMEM_BYTES = 60 * 2**20


def key_value_kernel(per, table, *refs):
    blocks, own, other = refs[:8], refs[8:10], refs[10:12]
    gain_ref, move_ref, x_out, out_ref, raw, x_all, w_all, x_sems, w_sems, out_sem = refs[12:]
    rows, depth = blocks[0].shape
    half = depth // 2
    core = table[16]
    for i in range(8):
        pltpu.make_async_copy(blocks[i], raw.at[i], x_sems.at[i]).start()
    start_weights(table, (8, 24), per, own, other, w_all, w_sems, depth)
    total = jnp.zeros((rows, 1), F32)
    for i in range(8):
        pltpu.make_async_copy(blocks[i], raw.at[i], x_sems.at[i]).wait()
        total += jnp.sum(raw[i].astype(F32), axis=1, keepdims=True)
    centre = total / (8 * depth)
    spread = jnp.zeros((rows, 1), F32)
    for i in range(8):
        spread += jnp.sum(jnp.square(raw[i].astype(F32) - centre), axis=1, keepdims=True)
    scale = lax.rsqrt(spread / (8 * depth) + 1e-06)
    total = None
    for lo, hi in PIECES:
        for i in range(lo, hi):
            for part, place in ((0, core), (1, 1 - core)):
                cols = pl.ds(pl.multiple_of(place * half, 128), half)
                value = (raw[i, :, cols].astype(F32) - centre) * scale
                value = value * (1.0 + gain_ref[table[i], :, cols]) + move_ref[table[i], :, cols]
                x_all[:, i * depth + part * half : i * depth + (part + 1) * half] = value.astype(BF16)
        for i in range(lo, hi):
            wait_weights(own, w_all, w_sems, depth, i)
        span = slice(lo * depth, hi * depth)
        prod = jnp.dot(x_all[:, span], w_all[span, :], preferred_element_type=F32)
        total = prod if total is None else total + prod
    copy = pltpu.make_async_copy(x_all, x_out, out_sem)
    copy.start()
    out_ref[...] = total.astype(BF16)
    copy.wait()


def key_value_rows(blocks, own_parts, other_parts, table, gains, moves):
    rows, depth = blocks[0].shape
    cols = own_parts[0].shape[2]
    vmem = pl.BlockSpec(memory_space=pltpu.VMEM)
    return pl.pallas_call(
        functools.partial(key_value_kernel, own_parts[0].shape[0]),
        in_specs=[pl.BlockSpec(memory_space=pltpu.SMEM)]
        + [pl.BlockSpec(memory_space=pl.ANY)] * 12
        + [vmem] * 2,
        out_specs=[pl.BlockSpec(memory_space=pl.ANY), vmem],
        out_shape=[
            jax.ShapeDtypeStruct((rows, 8 * depth), BF16),
            jax.ShapeDtypeStruct((rows, cols), BF16),
        ],
        scratch_shapes=[
            pltpu.VMEM((8, rows, depth), BF16),
            pltpu.VMEM((rows, 8 * depth), BF16),
            pltpu.VMEM((8 * depth, cols), BF16),
            pltpu.SemaphoreType.DMA((8,)),
            pltpu.SemaphoreType.DMA((8,)),
            pltpu.SemaphoreType.DMA,
        ],
        compiler_params=pltpu.CompilerParams(vmem_limit_bytes=VMEM_BYTES),
        name="key_value_rows",
    )(table, *blocks, *own_parts, *other_parts, gains, moves)


def query_kernel(table, x_ref, own, other, out_ref, x_all, w_all, x_sems, w_sems):
    depth = x_ref.shape[1] // 8
    start_weights(table, (0, 0), 8, [own], [other], w_all, w_sems, depth)

    def x_copy(i):
        cols = pl.ds(i * depth, depth)
        return pltpu.make_async_copy(x_ref.at[:, cols], x_all.at[:, cols], x_sems.at[i])

    for i in range(8):
        x_copy(i).start()
    total = None
    for lo, hi in PIECES:
        for i in range(lo, hi):
            wait_weights([own], w_all, w_sems, depth, i)
            x_copy(i).wait()
        span = slice(lo * depth, hi * depth)
        prod = jnp.dot(x_all[:, span], w_all[span, :], preferred_element_type=F32)
        total = prod if total is None else total + prod
    out_ref[...] = total.astype(BF16)


def query_rows(x_all, own, other, table):
    rows, width = x_all.shape
    cols = own.shape[2]
    return pl.pallas_call(
        query_kernel,
        in_specs=[pl.BlockSpec(memory_space=pltpu.SMEM)] + [pl.BlockSpec(memory_space=pl.ANY)] * 3,
        out_specs=pl.BlockSpec(memory_space=pltpu.VMEM),
        out_shape=jax.ShapeDtypeStruct((rows, cols), BF16),
        scratch_shapes=[
            pltpu.VMEM((rows, width), BF16),
            pltpu.VMEM((width, cols), BF16),
            pltpu.SemaphoreType.DMA((8,)),
            pltpu.SemaphoreType.DMA((8,)),
        ],
        compiler_params=pltpu.CompilerParams(vmem_limit_bytes=VMEM_BYTES),
        name="query_rows",
    )(table, x_all, own, other)


def attend_kernel(heads, *refs):
    sources, (out_ref, q_ref, prev_ref, own_ref, next_ref, bias_ref, sems) = refs[:5], refs[5:]
    copies = [
        pltpu.make_async_copy(source, target, sems.at[i])
        for i, (source, target) in enumerate(zip(sources, (q_ref, prev_ref, own_ref, next_ref, bias_ref)))
    ]
    for copy in copies:
        copy.start()
    for copy in copies:
        copy.wait()
    width = heads * HD
    row_len = PER_ROW * TILE
    for head in range(heads):
        cols = slice(head * HD, (head + 1) * HD)
        v_cols = slice(width + head * HD, width + (head + 1) * HD)
        for row in range(PER_LAYER // PER_ROW):
            lo = max(row - 1, 0) * row_len
            hi = min(row + 2, PER_LAYER // PER_ROW) * row_len
            queries = q_ref[row * row_len : (row + 1) * row_len, cols]
            scores = []
            for block, ref in enumerate((prev_ref, own_ref, next_ref)):
                part = lax.dot_general(
                    queries,
                    ref[lo:hi, cols],
                    (((1,), (1,)), ((), ())),
                    preferred_element_type=F32,
                ) * HD ** (-0.5)
                tiles = bias_ref[row * PER_ROW : (row + 1) * PER_ROW, block * LAYER + lo : block * LAYER + hi]
                part = part.reshape(PER_ROW, TILE, hi - lo) + tiles[:, None, :]
                scores.append(part.reshape(row_len, hi - lo))
            peak = functools.reduce(
                jnp.maximum, [jnp.max(part, axis=1, keepdims=True) for part in scores]
            )
            chances = [jnp.exp(part - peak) for part in scores]
            denom = sum(jnp.sum(part, axis=1, keepdims=True) for part in chances)
            total = sum(
                jnp.dot(part.astype(BF16), ref[lo:hi, v_cols], preferred_element_type=F32)
                for part, ref in zip(chances, (prev_ref, own_ref, next_ref))
            )
            out_ref[row * row_len : (row + 1) * row_len, cols] = (total / denom).astype(BF16)


def attend(*arrays):
    queries = arrays[0]
    heads = queries.shape[1] // HD
    return pl.pallas_call(
        functools.partial(attend_kernel, heads),
        in_specs=[pl.BlockSpec(memory_space=pl.ANY)] * 5,
        out_specs=pl.BlockSpec(memory_space=pltpu.VMEM),
        out_shape=jax.ShapeDtypeStruct(queries.shape, BF16),
        scratch_shapes=[pltpu.VMEM(array.shape, array.dtype) for array in arrays]
        + [pltpu.SemaphoreType.DMA((5,))],
        compiler_params=pltpu.CompilerParams(vmem_limit_bytes=VMEM_BYTES),
        name="attend",
    )(*arrays)


def output_kernel(first, count, last, table, *refs):
    parts, (own, other), rest = refs[:count], refs[count : count + 2], refs[count + 2 :]
    if last:
        sum_ref, res_ref, gate_ref, out_ref, x_all, w_all, sems = rest
    else:
        out_ref, x_all, w_all, sems = rest
    core = table[16]
    depth, half = own.shape[1:]

    def pairs(i):
        yield parts[i], x_all.at[:, pl.ds(i * depth, depth)]
        for ref, place in ((own, core), (other, 1 - core)):
            cols = pl.ds(pl.multiple_of(place * half, 128), half)
            yield ref.at[table[first + i]], w_all.at[pl.ds(i * depth, depth), cols]

    for i in range(count):
        for source, target in pairs(i):
            pltpu.make_async_copy(source, target, sems.at[i]).start()
    total = sum_ref[...] if last else None
    for lo in range(0, count, 2):
        hi = min(lo + 2, count)
        for i in range(lo, hi):
            for source, target in pairs(i):
                pltpu.make_async_copy(source, target, sems.at[i]).wait()
        span = slice(lo * depth, hi * depth)
        prod = jnp.dot(x_all[:, span], w_all[span, :], preferred_element_type=F32)
        total = prod if total is None else total + prod
    if last:
        total = res_ref[...].astype(F32) + gate_ref[...] * total
    out_ref[...] = total.astype(out_ref.dtype)


def output_rows(parts, first, own, other, table, last=()):
    count = len(parts)
    rows = parts[0].shape[0]
    depth = own.shape[1]
    cols = 2 * own.shape[2]
    vmem = pl.BlockSpec(memory_space=pltpu.VMEM)
    return pl.pallas_call(
        functools.partial(output_kernel, first, count, bool(last)),
        in_specs=[pl.BlockSpec(memory_space=pltpu.SMEM)]
        + [pl.BlockSpec(memory_space=pl.ANY)] * (count + 2)
        + [vmem] * len(last),
        out_specs=vmem,
        out_shape=jax.ShapeDtypeStruct((rows, cols), BF16 if last else F32),
        scratch_shapes=[
            pltpu.VMEM((rows, count * depth), BF16),
            pltpu.VMEM((count * depth, cols), BF16),
            pltpu.SemaphoreType.DMA((count,)),
        ],
        compiler_params=pltpu.CompilerParams(vmem_limit_bytes=VMEM_BYTES),
        name="output_rows",
    )(table, *parts, own, other, *last)


def stack_kernel(places, *refs):
    blocks, out_ref, sems = refs[:-2], refs[-2], refs[-1]
    copies = []
    for block, (source, target) in zip(blocks, places):
        source = block if source is None else block.at[source]
        target = out_ref.at[target[0], pl.ds(target[1], source.shape[0])]
        copies.append(pltpu.make_async_copy(source, target, sems.at[len(copies)]))
    for copy in copies:
        copy.start()
    for copy in copies:
        copy.wait()


def stack(blocks, places, shape):
    return pl.pallas_call(
        functools.partial(stack_kernel, places),
        in_specs=[pl.BlockSpec(memory_space=pl.ANY)] * len(blocks),
        out_specs=pl.BlockSpec(memory_space=pltpu.VMEM),
        out_shape=jax.ShapeDtypeStruct(shape, blocks[0].dtype),
        scratch_shapes=[pltpu.SemaphoreType.DMA((len(blocks),))],
        name="stack",
    )(*blocks)


def places():
    rows = np.zeros((128, 32), np.int32)
    for tile in range(16):
        for hid in range(8):
            x, yl, yh, z, c = hid // 2, hid % 2, tile // 8, tile // 2 % 4, tile % 2
            row = rows[tile * 8 + hid]
            row[:8] = [(x + s) % 4 * 2 + (yl ^ k) for k in range(2) for s in (0, -way(c), way(c), 2)]
            for first, w in ((8, way(c)), (24, -way(c))):
                pairs = [(yh ^ k) * 4 + (z + s) % 4 for k in range(2) for s in (0, -w, w, 2)]
                pairs = [pairs[i] for i in (0, 1, 2, 4, 5, 6, 3, 7)]
                row[first : first + 8] = [pairs.index(hid_of) for hid_of in row[:8]]
            row[16] = c
    return rows


def body(
    residual_in, w_query, w_key, w_value, w_output, shift_mod, scale_mod, gate_mod, neighbours
):
    tok_rows, feat_cols = residual_in.shape
    tile_id, hid_id = lax.axis_index("tile"), lax.axis_index("hid")
    table = lax.dynamic_index_in_dim(jnp.asarray(places()), tile_id * 8 + hid_id, 0, keepdims=False)
    pair_groups = [[p * 2 + c for p in range(8)] for c in range(2)]

    w_kv = jnp.concatenate([w_key, w_value], axis=1)
    w_rows, w_cols = w_kv.shape
    w_half = w_rows // 2
    x_a, x_b, w_a, w_b, w_mate, own, w_kv, w_q = lax.optimization_barrier(
        (
            send(residual_in, X_A),
            send(residual_in, X_B),
            send(w_kv, Z_A),
            send(w_kv, Z_B),
            send(w_kv, Y_HI),
            residual_in,
            w_kv,
            w_query,
        )
    )

    q_own = lax.all_gather(w_q[None], "tile", axis=0, axis_index_groups=pair_groups, tiled=True)
    early = stack([w_kv, w_a, w_b, w_mate], [(None, (i, 0)) for i in range(4)], (4, w_rows, w_cols))
    far, mate, w_mate_a, w_mate_b, early_other, x_a, x_b, w_a, w_b, own, early = (
        lax.optimization_barrier(
            (
                send(own, X_2),
                send(own, Y_LO),
                send(w_mate, Z_A),
                send(w_mate, Z_B),
                send(early, CORE),
                x_a,
                x_b,
                w_a,
                w_b,
                own,
                early,
            )
        )
    )

    mate_a = send(mate, X_A)
    mate_b = send(mate, X_B)
    mate_far = send(far, Y_LO)
    w_fwd_a = send(jnp.stack([w_a[:w_half], w_mate_a[:w_half]]), Z_A)
    w_fwd_b = send(jnp.stack([w_b[w_half:], w_mate_b[w_half:]]), Z_B)
    late = stack(
        [w_mate_a, w_mate_b, w_fwd_a, w_fwd_b, w_fwd_a, w_fwd_b],
        [(None, (0, 0)), (None, (1, 0)), (0, (2, 0)), (0, (2, w_half)), (1, (3, 0)), (1, (3, w_half))],
        (4, w_rows, w_cols),
    )
    late_other = send(late, CORE)
    mate_a, mate_b, mate_far, late, late_other, w_o = lax.optimization_barrier(
        (mate_a, mate_b, mate_far, late, late_other, w_output)
    )
    q_other = send(after(q_own, late_other), CORE)
    o_block = send(w_o, SWAP)

    listed = (neighbours >= 0).reshape(PER_LAYER, 3, 3, 3)
    grid = np.arange(PER_LAYER)
    row_step = grid[None, :] // PER_ROW - grid[:, None] // PER_ROW
    col_step = grid[None, :] % PER_ROW - grid[:, None] % PER_ROW
    bias = jnp.full((PER_LAYER, 3, PER_LAYER), -1e30, F32)
    for b in range(-1, 2):
        for e in range(-1, 2):
            here = jnp.asarray((row_step == b) & (col_step == e))[:, None, :]
            bias = jnp.where(here & listed[:, :, b + 1, e + 1][:, :, None], 0.0, bias)
    bias = jnp.repeat(bias.reshape(PER_LAYER, 3 * PER_LAYER), TILE, axis=1)

    x_all, key_value = key_value_rows(
        [own, x_a, x_b, far, mate, mate_a, mate_b, mate_far],
        [early, late],
        [early_other, late_other],
        table,
        scale_mod.reshape(8, 1, feat_cols),
        shift_mod.reshape(8, 1, feat_cols),
    )
    x_all, key_value, o_block = lax.optimization_barrier((x_all, key_value, o_block))
    o_own = lax.all_gather(o_block[None], "tile", axis=0, axis_index_groups=pair_groups, tiled=True)
    queries = query_rows(x_all, q_own, q_other, table)
    before, later, queries, key_value = lax.optimization_barrier(
        (send(key_value, NEXT), send(key_value, PREV), queries, key_value)
    )
    pieces = attend(queries, before, key_value, later, bias)

    p_a, p_b, p_far, p_mate, pieces = lax.optimization_barrier(
        (send(pieces, X_A), send(pieces, X_B), send(pieces, X_2), send(pieces, Y_LO), pieces)
    )
    o_other = send(after(o_own, p_a), CORE)
    p_mate_a = send(p_mate, X_A)
    p_mate_b = send(p_mate, X_B)
    p_mate_far = send(p_far, Y_LO)
    first = output_rows([pieces, p_a, p_b, p_far, p_mate], 0, o_own, o_other, table)
    gate = lax.dynamic_slice_in_dim(gate_mod, hid_id * feat_cols, feat_cols)[None]
    last = (first, residual_in, gate)
    return output_rows([p_mate_a, p_mate_b, p_mate_far], 5, o_own, o_other, table, last)


def solution(mesh):
    placed = (
        P("tile", "hid"),
        P("tile", "hid"),
        P("tile", "hid"),
        P("tile", "hid"),
        P("hid", "tile"),
        P(),
        P(),
        P(),
        P("tile", None),
    )
    return jax.shard_map(
        body, mesh=mesh, in_specs=placed, out_specs=P("tile", "hid"), check_vma=False
    )
```

```python
import functools

import jax
import jax.numpy as jnp
import numpy as np
from jax import lax
from jax.experimental import pallas as pl
from jax.experimental.pallas import tpu as pltpu
from jax.sharding import PartitionSpec as P

HD = 128
TILE = 32
PER_ROW = 4
PER_LAYER = 16
LAYER = PER_LAYER * TILE
AXES = ("tile", "hid")
F32 = jnp.float32
BF16 = jnp.bfloat16


def route(move):
    pairs = []
    for x in range(4):
        for yl in range(2):
            for yh in range(2):
                for z in range(4):
                    for c in range(2):
                        a, b, d, e, f = move(x, yl, yh, z, c)
                        source = (yh * 8 + z * 2 + c) * 8 + x * 2 + yl
                        target = (d * 8 + e % 4 * 2 + f) * 8 + a % 4 * 2 + b
                        pairs.append((source, target))
    return pairs


def way(c):
    return 1 - 2 * c


X_A = route(lambda x, yl, yh, z, c: (x + way(c), yl, yh, z, c))
X_B = route(lambda x, yl, yh, z, c: (x - way(c), yl, yh, z, c))
X_1 = route(lambda x, yl, yh, z, c: (x ^ 1, yl, yh, z, c))
X_2 = route(lambda x, yl, yh, z, c: (x + 2, yl, yh, z, c))
Z_A = route(lambda x, yl, yh, z, c: (x, yl, yh, z + way(c), c))
Z_2 = route(lambda x, yl, yh, z, c: (x, yl, yh, z + 2, c))
Z_B = route(lambda x, yl, yh, z, c: (x, yl, yh, z - way(c), c))
Y_LO = route(lambda x, yl, yh, z, c: (x, 1 - yl, yh, z, c))
Y_HI = route(lambda x, yl, yh, z, c: (x, yl, 1 - yh, z, c))
CORE = route(lambda x, yl, yh, z, c: (x, yl, yh, z, 1 - c))
SWAP = route(
    lambda x, yl, yh, z, c: (
        yh * 2 + z // 2,
        z % 2,
        yh ^ x // 2,
        z + x % 2 + 2 * (yl ^ z % 2),
        c,
    )
)


def rows_held(hid, pair):
    yh, z, ahead = hid // 4, hid % 4, (pair - hid) % 4
    return (pair // 4 ^ yh) * 4 + ahead % 2 * 2 + (z % 2 ^ ahead // 2)


NEXT = [(t * 8 + h, t * 8 + 8 + h) for t in range(15) for h in range(8)]
PREV = [(t * 8 + 8 + h, t * 8 + h) for t in range(15) for h in range(8)]


def send(array, pairs):
    return lax.ppermute(array, AXES, pairs)


def after(array, *others):
    return lax.optimization_barrier((array, *others))[0]


VMEM_BYTES = 60 * 2**20


def place_copies(place, parts, target, sem):
    stacked, singles = parts[0], [part for part in parts[1:] if not isinstance(part, tuple)]
    count, half = stacked.shape[0], target.shape[0] // 2
    last = count + len(singles)

    def copy(source, to):
        return pltpu.make_async_copy(source, to, sem)

    yield place < count, lambda: [copy(stacked.at[jnp.minimum(place, count - 1)], target)]
    for k, single in enumerate(singles):
        yield place == count + k, lambda single=single: [copy(single, target)]
    if isinstance(parts[-1], tuple):
        entry = jnp.maximum(place - last, 0)
        yield place >= last, lambda: [
            copy(ref.at[entry], target.at[pl.ds(k * half, half)]) for k, ref in enumerate(parts[-1])
        ]


def start_block(place, parts, target, sem):
    for here, copies in place_copies(place, parts, target, sem):

        @pl.when(here)
        def _():
            for copy in copies():
                copy.start()


def modulate_project_kernel(table, *refs):
    blocks, parts, refs = refs[:8], refs[8:11], refs[11:]
    gain_ref, move_ref, other_out, out_ref, raw, own, other, w_all, x_sems, w_sems, out_sem = refs
    rows, depth = blocks[0].shape
    half = depth // 2
    parts = [parts[0], (parts[1], parts[2])]
    for i in range(8):
        pltpu.make_async_copy(blocks[i], raw.at[i], x_sems.at[i]).start()
    for i in range(8):
        start_block(table[8 + i], parts, w_all.at[pl.ds(i * half, half), :], w_sems.at[i])
    total = jnp.zeros((rows, 1), F32)
    for i in range(8):
        pltpu.make_async_copy(blocks[i], raw.at[i], x_sems.at[i]).wait()
        total += jnp.sum(raw[i].astype(F32), axis=1, keepdims=True)
    centre = total / (8 * depth)
    spread = jnp.zeros((rows, 1), F32)
    for i in range(8):
        spread += jnp.sum(jnp.square(raw[i].astype(F32) - centre), axis=1, keepdims=True)
    scale = lax.rsqrt(spread / (8 * depth) + 1e-06)
    for i in range(8):
        value = (raw[i].astype(F32) - centre) * scale
        value = (value * (1.0 + gain_ref[table[i]]) + move_ref[table[i]]).astype(BF16)
        low, high = value[:, :half], value[:, half:]
        own[:, i * half : (i + 1) * half] = jnp.where(table[16] == 0, low, high)
        other[:, i * half : (i + 1) * half] = jnp.where(table[16] == 0, high, low)
    copy = pltpu.make_async_copy(other, other_out, out_sem)
    copy.start()
    for i in range(8):
        target = w_all.at[pl.ds(i * half, half), :]
        pltpu.make_async_copy(parts[0].at[0], target, w_sems.at[i]).wait()
    out_ref[...] = jnp.dot(own[...], w_all[...], preferred_element_type=F32)
    copy.wait()


def modulate_project(blocks, weights, table, gains, moves):
    rows, depth = blocks[0].shape
    cols = weights[0].shape[2]
    half = (rows, 4 * depth)
    vmem = pl.BlockSpec(memory_space=pltpu.VMEM)
    anywhere = pl.BlockSpec(memory_space=pl.ANY)
    return pl.pallas_call(
        modulate_project_kernel,
        in_specs=[pl.BlockSpec(memory_space=pltpu.SMEM)] + [anywhere] * 11 + [vmem] * 2,
        out_specs=[anywhere, vmem],
        out_shape=[jax.ShapeDtypeStruct(half, BF16), jax.ShapeDtypeStruct((rows, cols), F32)],
        scratch_shapes=[
            pltpu.VMEM((8, rows, depth), BF16),
            pltpu.VMEM(half, BF16),
            pltpu.VMEM(half, BF16),
            pltpu.VMEM((4 * depth, cols), BF16),
            pltpu.SemaphoreType.DMA((8,)),
            pltpu.SemaphoreType.DMA((8,)),
            pltpu.SemaphoreType.DMA,
        ],
        compiler_params=pltpu.CompilerParams(vmem_limit_bytes=VMEM_BYTES),
        name="modulate_project",
    )(table, *blocks, *weights, gains, moves)


def project_kernel(first_col, table, x_ref, *refs):
    parts, (add_ref, out_ref, x_all, w_all, sum_all, x_sems, w_sems, sum_sem) = refs[:3], refs[3:]
    depth = x_ref.shape[1] // 8
    cols = out_ref.shape[1]
    span = pl.ds(first_col, cols)
    parts = [part.at[:, :, span] for part in parts]
    parts = [parts[0], (parts[1], parts[2])]
    pieces = (0, 2, 5, 8)

    def x_copy(n):
        lo, hi = pieces[n], pieces[n + 1]
        here = pl.ds(lo * depth, (hi - lo) * depth)
        return pltpu.make_async_copy(x_ref.at[:, here], x_all.at[:, here], x_sems.at[n])

    def target(i):
        return w_all.at[pl.ds(i * depth, depth), :]

    for n in range(3):
        x_copy(n).start()
        for i in range(pieces[n], pieces[n + 1]):
            start_block(table[24 + i], parts, target(i), w_sems.at[i])
    sum_copy = pltpu.make_async_copy(add_ref.at[:, span], sum_all, sum_sem)
    sum_copy.start()
    total = None
    for n in range(3):
        x_copy(n).wait()
        for i in range(pieces[n], pieces[n + 1]):
            pltpu.make_async_copy(parts[0].at[0], target(i), w_sems.at[i]).wait()
        here = slice(pieces[n] * depth, pieces[n + 1] * depth)
        prod = jnp.dot(x_all[:, here], w_all[here, :], preferred_element_type=F32)
        total = prod if total is None else total + prod
    sum_copy.wait()
    out_ref[...] = (total + sum_all[...]).astype(BF16)


def project(x, weights, table, first_col, cols, add):
    rows, width = x.shape
    return pl.pallas_call(
        functools.partial(project_kernel, first_col),
        in_specs=[pl.BlockSpec(memory_space=pltpu.SMEM)] + [pl.BlockSpec(memory_space=pl.ANY)] * 5,
        out_specs=pl.BlockSpec(memory_space=pltpu.VMEM),
        out_shape=jax.ShapeDtypeStruct((rows, cols), BF16),
        scratch_shapes=[
            pltpu.VMEM((rows, width), BF16),
            pltpu.VMEM((width, cols), BF16),
            pltpu.VMEM((rows, cols), F32),
            pltpu.SemaphoreType.DMA((3,)),
            pltpu.SemaphoreType.DMA((8,)),
            pltpu.SemaphoreType.DMA,
        ],
        compiler_params=pltpu.CompilerParams(vmem_limit_bytes=VMEM_BYTES),
        name="project",
    )(table, x, *weights, add)


def attend_kernel(heads, *refs):
    sources, (out_ref, q_ref, prev_ref, own_ref, next_ref, bias_ref, sems) = refs[:5], refs[5:]
    copies = [
        pltpu.make_async_copy(source, target, sems.at[i])
        for i, (source, target) in enumerate(zip(sources, (q_ref, prev_ref, own_ref, next_ref, bias_ref)))
    ]
    for copy in copies:
        copy.start()
    for copy in copies:
        copy.wait()
    width = heads * HD
    row_len = PER_ROW * TILE
    for head in range(heads):
        cols = slice(head * HD, (head + 1) * HD)
        v_cols = slice(width + head * HD, width + (head + 1) * HD)
        for row in range(PER_LAYER // PER_ROW):
            lo = max(row - 1, 0) * row_len
            hi = min(row + 2, PER_LAYER // PER_ROW) * row_len
            queries = q_ref[row * row_len : (row + 1) * row_len, cols]
            scores = []
            for block, ref in enumerate((prev_ref, own_ref, next_ref)):
                part = lax.dot_general(
                    queries,
                    ref[lo:hi, cols],
                    (((1,), (1,)), ((), ())),
                    preferred_element_type=F32,
                ) * HD ** (-0.5)
                tiles = bias_ref[row * PER_ROW : (row + 1) * PER_ROW, block * LAYER + lo : block * LAYER + hi]
                part = part.reshape(PER_ROW, TILE, hi - lo) + tiles[:, None, :]
                scores.append(part.reshape(row_len, hi - lo))
            peak = functools.reduce(
                jnp.maximum, [jnp.max(part, axis=1, keepdims=True) for part in scores]
            )
            chances = [jnp.exp(part - peak) for part in scores]
            denom = sum(jnp.sum(part, axis=1, keepdims=True) for part in chances)
            total = sum(
                jnp.dot(part.astype(BF16), ref[lo:hi, v_cols], preferred_element_type=F32)
                for part, ref in zip(chances, (prev_ref, own_ref, next_ref))
            )
            out_ref[row * row_len : (row + 1) * row_len, cols] = (total / denom).astype(BF16)


def attend(*arrays):
    queries = arrays[0]
    heads = queries.shape[1] // HD
    return pl.pallas_call(
        functools.partial(attend_kernel, heads),
        in_specs=[pl.BlockSpec(memory_space=pl.ANY)] * 5,
        out_specs=pl.BlockSpec(memory_space=pltpu.VMEM),
        out_shape=jax.ShapeDtypeStruct(queries.shape, BF16),
        scratch_shapes=[pltpu.VMEM(array.shape, array.dtype) for array in arrays]
        + [pltpu.SemaphoreType.DMA((5,))],
        compiler_params=pltpu.CompilerParams(vmem_limit_bytes=VMEM_BYTES),
        name="attend",
    )(*arrays)


def output_kernel(first, count, last, table, *refs):
    parts, own, other, rest = refs[:count], refs[count : count + 4], refs[count + 4 : count + 8], refs[count + 8 :]
    if last:
        sum_ref, res_ref, gate_ref, out_ref, x_all, w_all, sems, sum_all, res_all, sum_sems = rest
        sum_copies = [
            pltpu.make_async_copy(sum_ref, sum_all, sum_sems.at[0]),
            pltpu.make_async_copy(res_ref, res_all, sum_sems.at[1]),
        ]
    else:
        out_ref, x_all, w_all, sems = rest
        sum_copies = []
    core = table[16]
    depth, half = own[0].shape[1:]

    def x_copy(i):
        return pltpu.make_async_copy(parts[i], x_all.at[:, pl.ds(i * depth, depth)], sems.at[i])

    def target(i, place):
        cols = pl.ds(pl.multiple_of(place * half, 128), half)
        return w_all.at[pl.ds(i * depth, depth), cols]

    for i in range(count):
        x_copy(i).start()
        for base, refs_of, place in ((32, own, core), (40, other, 1 - core)):
            start_block(table[base + first + i], refs_of, target(i, place), sems.at[i])

    for copy in sum_copies:
        copy.start()
    total = None
    for lo in range(0, count, 2):
        hi = min(lo + 2, count)
        for i in range(lo, hi):
            x_copy(i).wait()
            for place in range(2):
                pltpu.make_async_copy(own[0].at[0], target(i, place), sems.at[i]).wait()
        span = slice(lo * depth, hi * depth)
        prod = jnp.dot(x_all[:, span], w_all[span, :], preferred_element_type=F32)
        total = prod if total is None else total + prod
    if last:
        for copy in sum_copies:
            copy.wait()
        total = res_all[...].astype(F32) + gate_ref[...] * (total + sum_all[...])
    out_ref[...] = total.astype(out_ref.dtype)


def output_rows(parts, first, own, other, table, last=()):
    count = len(parts)
    rows, depth = parts[0].shape
    cols = 2 * own[0].shape[2]
    vmem = pl.BlockSpec(memory_space=pltpu.VMEM)
    anywhere = pl.BlockSpec(memory_space=pl.ANY)
    scratch = [
        pltpu.VMEM((rows, count * depth), BF16),
        pltpu.VMEM((count * depth, cols), BF16),
        pltpu.SemaphoreType.DMA((count,)),
    ]
    if last:
        scratch += [
            pltpu.VMEM((rows, cols), F32),
            pltpu.VMEM((rows, cols), BF16),
            pltpu.SemaphoreType.DMA((2,)),
        ]
    return pl.pallas_call(
        functools.partial(output_kernel, first, count, bool(last)),
        in_specs=[pl.BlockSpec(memory_space=pltpu.SMEM)]
        + [anywhere] * (count + 8)
        + ([anywhere, anywhere, vmem] if last else []),
        out_specs=vmem,
        out_shape=jax.ShapeDtypeStruct((rows, cols), BF16 if last else F32),
        scratch_shapes=scratch,
        compiler_params=pltpu.CompilerParams(vmem_limit_bytes=VMEM_BYTES),
        name="output_rows",
    )(table, *parts, *own, *other, *last)


def stack_kernel(axis, *refs):
    blocks, out_ref, sems = refs[:-2], refs[-2], refs[-1]
    copies = []
    for i, block in enumerate(blocks):
        cols = block.shape[-1]
        target = out_ref.at[i] if axis == 0 else out_ref.at[:, pl.ds(i * cols, cols)]
        copies.append(pltpu.make_async_copy(block, target, sems.at[i]))
    for copy in copies:
        copy.start()
    for copy in copies:
        copy.wait()


def stack(blocks, axis=0):
    rows, cols = blocks[0].shape
    shape = (len(blocks), rows, cols) if axis == 0 else (rows, len(blocks) * cols)
    return pl.pallas_call(
        functools.partial(stack_kernel, axis),
        in_specs=[pl.BlockSpec(memory_space=pl.ANY)] * len(blocks),
        out_specs=pl.BlockSpec(memory_space=pltpu.VMEM),
        out_shape=jax.ShapeDtypeStruct(shape, blocks[0].dtype),
        scratch_shapes=[pltpu.SemaphoreType.DMA((len(blocks),))],
        name="stack",
    )(*blocks)


def places():
    rows = np.zeros((128, 48), np.int32)
    for tile in range(16):
        for hid in range(8):
            x, yl, yh, z, c = hid // 2, hid % 2, tile // 8, tile // 2 % 4, tile % 2
            row = rows[tile * 8 + hid]
            row[:8] = [(x + s) % 4 * 2 + (yl ^ k) for k in range(2) for s in (0, -way(c), way(c), 2)]
            row[16] = c
            for first, w in ((8, way(c)), (24, -way(c)), (32, way(c)), (40, -way(c))):
                pairs = [(yh ^ k) * 4 + (z + s) % 4 for k in range(2) for s in (0, -w, w, 2)]
                if first < 32:
                    pairs = [pairs[i] for i in (0, 1, 2, 4, 5, 6, 3, 7)]
                else:
                    pairs = [rows_held(hid, pair) for pair in pairs]
                row[first : first + 8] = [pairs.index(hid_of) for hid_of in row[:8]]
    return rows


def body(
    residual_in, w_query, w_key, w_value, w_output, shift_mod, scale_mod, gate_mod, neighbours
):
    tok_rows, feat_cols = residual_in.shape
    tile_id, hid_id = lax.axis_index("tile"), lax.axis_index("hid")
    table = lax.dynamic_index_in_dim(jnp.asarray(places()), tile_id * 8 + hid_id, 0, keepdims=False)

    listed = (neighbours >= 0).reshape(PER_LAYER, 3, 3, 3)
    grid = np.arange(PER_LAYER)
    row_step = grid[None, :] // PER_ROW - grid[:, None] // PER_ROW
    col_step = grid[None, :] % PER_ROW - grid[:, None] % PER_ROW
    bias = jnp.full((PER_LAYER, 3, PER_LAYER), -1e30, F32)
    for b in range(-1, 2):
        for e in range(-1, 2):
            here = jnp.asarray((row_step == b) & (col_step == e))[:, None, :]
            bias = jnp.where(here & listed[:, :, b + 1, e + 1][:, :, None], 0.0, bias)
    bias = jnp.repeat(bias.reshape(PER_LAYER, 3 * PER_LAYER), TILE, axis=1)

    gate = lax.dynamic_slice_in_dim(gate_mod, hid_id * feat_cols, feat_cols)[None]

    fence = lax.optimization_barrier
    weights = stack([w_key, w_value, w_query], axis=1)
    kv_cols = 2 * w_key.shape[1]
    w_rows, w_cols = weights.shape
    w_half = w_rows // 2
    x_a, x_b, w_a, w_b, w_mate, own, weights, bias, table, gate, o_block = fence(
        (
            send(residual_in, X_A),
            send(residual_in, X_B),
            send(weights, Z_A),
            send(weights, Z_B),
            send(weights, Y_HI),
            residual_in,
            weights,
            bias,
            table,
            gate,
            w_output,
        )
    )

    far, mate, w_mate_a, w_mate_b, x_a, x_b, w_a, w_b, own, w_mate, weights = fence(
        (
            send(own, X_2),
            send(own, Y_LO),
            send(w_mate, Z_A),
            send(w_mate, Z_B),
            x_a,
            x_b,
            w_a,
            w_b,
            own,
            w_mate,
            weights,
        )
    )

    mate_a, mate_b, mate_far, w_fwd_a, w_fwd_b, early, o_block = fence(
        (
            send(mate, X_A),
            send(mate, X_B),
            send(far, Y_LO),
            send(jnp.stack([w_a[:w_half], w_mate_a[:w_half]]), Z_A),
            send(jnp.stack([w_b[w_half:], w_mate_b[w_half:]]), Z_B),
            stack([weights, w_a, w_b, w_mate, w_mate_a, w_mate_b]),
            o_block,
        )
    )

    mine = [early, w_fwd_a, w_fwd_b]
    x_other, first = modulate_project(
        [own, x_a, x_b, far, mate, mate_a, mate_b, mate_far],
        mine,
        table,
        scale_mod.reshape(8, 1, feat_cols),
        shift_mod.reshape(8, 1, feat_cols),
    )
    first, x_other, o_block, *theirs = fence(
        (first, x_other, send(o_block, SWAP), *[send(part, CORE) for part in mine])
    )

    key_value = project(x_other, theirs, table, 0, kv_cols, first)
    key_value, o_block, o_a, o_b, o_far, o_mate, first, x_other, *theirs = fence(
        (
            key_value,
            o_block,
            send(o_block, Z_A),
            send(o_block, Z_B),
            send(o_block, Z_2),
            send(o_block, Y_HI),
            first,
            x_other,
            *theirs,
        )
    )

    queries = project(x_other, theirs, table, kv_cols, w_cols - kv_cols, first)
    before, later, queries, key_value, o_mate_a, o_mate_b, o_early, o_mate = fence(
        (
            send(key_value, NEXT),
            send(key_value, PREV),
            queries,
            key_value,
            send(o_mate, Z_A),
            send(o_mate, Z_B),
            stack([o_block, o_a, o_b, o_far, o_mate]),
            o_mate,
        )
    )

    pieces = attend(queries, before, key_value, later, bias)
    pieces, o_mate_far, *both = fence(
        (
            pieces,
            send(o_mate, Z_2),
            *[send(part, CORE) for part in (o_early, o_mate_a, o_mate_b)],
            o_early,
            o_mate_a,
            o_mate_b,
        )
    )
    o_mine = [*both[3:], o_mate_far]

    p_a, p_b, p_far, p_mate, pieces, o_last = fence(
        (
            send(pieces, X_A),
            send(pieces, X_B),
            send(pieces, X_2),
            send(pieces, Y_LO),
            pieces,
            send(o_mate_far, CORE),
        )
    )
    o_theirs = [*both[:3], o_last]
    p_mate_a = send(p_mate, X_A)
    p_mate_b = send(p_mate, X_B)
    p_mate_far = send(p_far, Y_LO)
    near = output_rows([pieces, p_a, p_b, p_far, p_mate], 0, o_mine, o_theirs, table)
    last = (near, residual_in, gate)
    return output_rows([p_mate_a, p_mate_b, p_mate_far], 5, o_mine, o_theirs, table, last)


def solution(mesh):
    placed = (
        P("tile", "hid"),
        P("tile", "hid"),
        P("tile", "hid"),
        P("tile", "hid"),
        P("hid", "tile"),
        P(),
        P(),
        P(),
        P("tile", None),
    )
    return jax.shard_map(
        body, mesh=mesh, in_specs=placed, out_specs=P("tile", "hid"), check_vma=False
    )
```

```python
import functools

import jax
import jax.numpy as jnp
import numpy as np
from jax import lax
from jax.experimental import pallas as pl
from jax.experimental.pallas import tpu as pltpu
from jax.sharding import PartitionSpec as P

HD = 128
TILE = 32
PER_ROW = 4
PER_LAYER = 16
LAYER = PER_LAYER * TILE
AXES = ("tile", "hid")
F32 = jnp.float32
BF16 = jnp.bfloat16


def route(move):
    pairs = []
    for x in range(4):
        for yl in range(2):
            for yh in range(2):
                for z in range(4):
                    for c in range(2):
                        a, b, d, e, f = move(x, yl, yh, z, c)
                        source = (yh * 8 + z * 2 + c) * 8 + x * 2 + yl
                        target = (d * 8 + e % 4 * 2 + f) * 8 + a % 4 * 2 + b
                        pairs.append((source, target))
    return pairs


def way(c):
    return 1 - 2 * c


X_A = route(lambda x, yl, yh, z, c: (x + way(c), yl, yh, z, c))
X_B = route(lambda x, yl, yh, z, c: (x - way(c), yl, yh, z, c))
X_1 = route(lambda x, yl, yh, z, c: (x ^ 1, yl, yh, z, c))
X_2 = route(lambda x, yl, yh, z, c: (x + 2, yl, yh, z, c))
Z_A = route(lambda x, yl, yh, z, c: (x, yl, yh, z + way(c), c))
Z_2 = route(lambda x, yl, yh, z, c: (x, yl, yh, z + 2, c))
Z_B = route(lambda x, yl, yh, z, c: (x, yl, yh, z - way(c), c))
Y_LO = route(lambda x, yl, yh, z, c: (x, 1 - yl, yh, z, c))
Y_HI = route(lambda x, yl, yh, z, c: (x, yl, 1 - yh, z, c))
CORE = route(lambda x, yl, yh, z, c: (x, yl, yh, z, 1 - c))
SWAP_1 = route(lambda x, yl, yh, z, c: (x, yl, yh ^ x // 2, z + 2 * (x % 2) + yl, c))


def second_move(x, yl, yh, z, c):
    from_z = (z - 2 * (x % 2) - yl) % 4
    return 2 * (yh ^ x // 2) + from_z // 2, from_z % 2, yh, z, c


SWAP_2 = route(second_move)


def rows_held(hid, pair):
    return (pair // 4 ^ hid // 4) * 4 + (pair - hid) % 4


NEXT = [(t * 8 + h, t * 8 + 8 + h) for t in range(15) for h in range(8)]
PREV = [(t * 8 + 8 + h, t * 8 + h) for t in range(15) for h in range(8)]


def send(array, pairs):
    return lax.ppermute(array, AXES, pairs)


def after(array, *others):
    return lax.optimization_barrier((array, *others))[0]


VMEM_BYTES = 60 * 2**20


def place_copies(place, parts, target, sem):
    half = target.shape[0] // 2
    first = 0
    for part in parts:
        refs = part if isinstance(part, tuple) else (part,)
        count = refs[0].shape[0] if len(refs[0].shape) == 3 else 1
        entry = jnp.clip(place - first, 0, count - 1)
        here = (place >= first) & (place < first + count)
        if len(refs) == 1:
            source = part.at[entry] if len(part.shape) == 3 else part
            yield here, [pltpu.make_async_copy(source, target, sem)]
        else:
            yield here, [
                pltpu.make_async_copy(ref.at[entry], target.at[pl.ds(k * half, half)], sem)
                for k, ref in enumerate(refs)
            ]
        first += count


def start_block(place, parts, target, sem):
    for here, copies in place_copies(place, parts, target, sem):

        @pl.when(here)
        def _():
            for copy in copies:
                copy.start()


def modulate_project_kernel(table, *refs):
    blocks, parts, refs = refs[:8], refs[8:11], refs[11:]
    gain_ref, move_ref, other_out, out_ref, raw, own, other, w_all, x_sems, w_sems, out_sem = refs
    rows, depth = blocks[0].shape
    half = depth // 2
    parts = [parts[0], (parts[1], parts[2])]
    for i in range(8):
        pltpu.make_async_copy(blocks[i], raw.at[i], x_sems.at[i]).start()

    def fold(value):
        return sum(value[:, lane : lane + 128] for lane in range(0, depth, 128))

    total = jnp.zeros((rows, 128), F32)
    for i in range(8):
        pltpu.make_async_copy(blocks[i], raw.at[i], x_sems.at[i]).wait()
        total += fold(raw[i].astype(F32))
    for i in range(8):
        start_block(table[8 + i], parts, w_all.at[pl.ds(i * half, half), :], w_sems.at[i])
    centre = jnp.sum(total, axis=1, keepdims=True) / (8 * depth)
    spread = jnp.zeros((rows, 128), F32)
    for i in range(8):
        spread += fold(jnp.square(raw[i].astype(F32) - centre))
    scale = lax.rsqrt(jnp.sum(spread, axis=1, keepdims=True) / (8 * depth) + 1e-06)

    def modulate(low_ref, high_ref):
        for i in range(8):
            value = (raw[i].astype(F32) - centre) * scale
            value = (value * (1.0 + gain_ref[table[i]]) + move_ref[table[i]]).astype(BF16)
            low_ref[:, i * half : (i + 1) * half] = value[:, :half]
            high_ref[:, i * half : (i + 1) * half] = value[:, half:]

    @pl.when(table[16] == 0)
    def _():
        modulate(own, other)

    @pl.when(table[16] == 1)
    def _():
        modulate(other, own)

    copy = pltpu.make_async_copy(other, other_out, out_sem)
    copy.start()
    for i in range(8):
        target = w_all.at[pl.ds(i * half, half), :]
        pltpu.make_async_copy(parts[0].at[0], target, w_sems.at[i]).wait()
    out_ref[...] = jnp.dot(own[...], w_all[...], preferred_element_type=F32)
    copy.wait()


def modulate_project(blocks, weights, table, gains, moves):
    rows, depth = blocks[0].shape
    cols = weights[0].shape[2]
    half = (rows, 4 * depth)
    vmem = pl.BlockSpec(memory_space=pltpu.VMEM)
    anywhere = pl.BlockSpec(memory_space=pl.ANY)
    return pl.pallas_call(
        modulate_project_kernel,
        in_specs=[pl.BlockSpec(memory_space=pltpu.SMEM)] + [anywhere] * 11 + [vmem] * 2,
        out_specs=[anywhere, vmem],
        out_shape=[jax.ShapeDtypeStruct(half, BF16), jax.ShapeDtypeStruct((rows, cols), F32)],
        scratch_shapes=[
            pltpu.VMEM((8, rows, depth), BF16),
            pltpu.VMEM(half, BF16),
            pltpu.VMEM(half, BF16),
            pltpu.VMEM((4 * depth, cols), BF16),
            pltpu.SemaphoreType.DMA((8,)),
            pltpu.SemaphoreType.DMA((8,)),
            pltpu.SemaphoreType.DMA,
        ],
        compiler_params=pltpu.CompilerParams(vmem_limit_bytes=VMEM_BYTES),
        name="modulate_project",
    )(table, *blocks, *weights, gains, moves)


def project_kernel(first_col, table, x_ref, *refs):
    parts, (add_ref, out_ref, x_all, w_all, sum_all, x_sems, w_sems, sum_sem) = refs[:3], refs[3:]
    depth = x_ref.shape[1] // 8
    cols = out_ref.shape[1]
    span = pl.ds(first_col, cols)
    parts = [part.at[:, :, span] for part in parts]
    parts = [parts[0], (parts[1], parts[2])]
    pieces = (0, 2, 5, 8)

    def x_copy(n):
        lo, hi = pieces[n], pieces[n + 1]
        here = pl.ds(lo * depth, (hi - lo) * depth)
        return pltpu.make_async_copy(x_ref.at[:, here], x_all.at[:, here], x_sems.at[n])

    def target(i):
        return w_all.at[pl.ds(i * depth, depth), :]

    def start(n):
        x_copy(n).start()
        for i in range(pieces[n], pieces[n + 1]):
            start_block(table[24 + i], parts, target(i), w_sems.at[i])

    sum_copy = pltpu.make_async_copy(add_ref.at[:, span], sum_all, sum_sem)
    start(0)
    start(1)
    total = None
    for n in range(3):
        x_copy(n).wait()
        for i in range(pieces[n], pieces[n + 1]):
            pltpu.make_async_copy(parts[0].at[0], target(i), w_sems.at[i]).wait()
        if n == 0:
            start(2)
            sum_copy.start()
        here = slice(pieces[n] * depth, pieces[n + 1] * depth)
        prod = jnp.dot(x_all[:, here], w_all[here, :], preferred_element_type=F32)
        total = prod if total is None else total + prod
    sum_copy.wait()
    out_ref[...] = (total + sum_all[...]).astype(BF16)


def project(x, weights, table, first_col, cols, add):
    rows, width = x.shape
    return pl.pallas_call(
        functools.partial(project_kernel, first_col),
        in_specs=[pl.BlockSpec(memory_space=pltpu.SMEM)] + [pl.BlockSpec(memory_space=pl.ANY)] * 5,
        out_specs=pl.BlockSpec(memory_space=pltpu.VMEM),
        out_shape=jax.ShapeDtypeStruct((rows, cols), BF16),
        scratch_shapes=[
            pltpu.VMEM((rows, width), BF16),
            pltpu.VMEM((width, cols), BF16),
            pltpu.VMEM((rows, cols), F32),
            pltpu.SemaphoreType.DMA((3,)),
            pltpu.SemaphoreType.DMA((8,)),
            pltpu.SemaphoreType.DMA,
        ],
        compiler_params=pltpu.CompilerParams(vmem_limit_bytes=VMEM_BYTES),
        name="project",
    )(table, x, *weights, add)


def attend_kernel(heads, *refs):
    sources, (out_ref, q_ref, prev_ref, own_ref, next_ref, bias_ref, sems) = refs[:5], refs[5:]
    copies = [
        pltpu.make_async_copy(source, target, sems.at[i])
        for i, (source, target) in enumerate(zip(sources, (q_ref, prev_ref, own_ref, next_ref, bias_ref)))
    ]
    for copy in copies:
        copy.start()
    for copy in copies:
        copy.wait()
    width = heads * HD
    row_len = PER_ROW * TILE
    for head in range(heads):
        cols = slice(head * HD, (head + 1) * HD)
        v_cols = slice(width + head * HD, width + (head + 1) * HD)
        for row in range(PER_LAYER // PER_ROW):
            lo = max(row - 1, 0) * row_len
            hi = min(row + 2, PER_LAYER // PER_ROW) * row_len
            queries = q_ref[row * row_len : (row + 1) * row_len, cols]
            scores = []
            for block, ref in enumerate((prev_ref, own_ref, next_ref)):
                part = lax.dot_general(
                    queries,
                    ref[lo:hi, cols],
                    (((1,), (1,)), ((), ())),
                    preferred_element_type=F32,
                ) * HD ** (-0.5)
                tiles = bias_ref[row * PER_ROW : (row + 1) * PER_ROW, block * LAYER + lo : block * LAYER + hi]
                part = part.reshape(PER_ROW, TILE, hi - lo) + tiles[:, None, :]
                scores.append(part.reshape(row_len, hi - lo))
            peak = functools.reduce(
                jnp.maximum, [jnp.max(part, axis=1, keepdims=True) for part in scores]
            )
            chances = [jnp.exp(part - peak) for part in scores]
            denom = sum(jnp.sum(part, axis=1, keepdims=True) for part in chances)
            total = sum(
                jnp.dot(part.astype(BF16), ref[lo:hi, v_cols], preferred_element_type=F32)
                for part, ref in zip(chances, (prev_ref, own_ref, next_ref))
            )
            out_ref[row * row_len : (row + 1) * row_len, cols] = (total / denom).astype(BF16)


def attend(*arrays):
    queries = arrays[0]
    heads = queries.shape[1] // HD
    return pl.pallas_call(
        functools.partial(attend_kernel, heads),
        in_specs=[pl.BlockSpec(memory_space=pl.ANY)] * 5,
        out_specs=pl.BlockSpec(memory_space=pltpu.VMEM),
        out_shape=jax.ShapeDtypeStruct(queries.shape, BF16),
        scratch_shapes=[pltpu.VMEM(array.shape, array.dtype) for array in arrays]
        + [pltpu.SemaphoreType.DMA((5,))],
        compiler_params=pltpu.CompilerParams(vmem_limit_bytes=VMEM_BYTES),
        name="attend",
    )(*arrays)


def output_kernel(first, count, table, *refs):
    parts, own, other = refs[:count], refs[count : count + 4], refs[count + 4 : count + 8]
    sum_ref, gate_ref, out_ref, x_all, w_all, sum_all, sems, sum_sem = refs[count + 8 :]
    sum_copy = pltpu.make_async_copy(sum_ref, sum_all, sum_sem)
    sum_copy.start()
    core = table[16]
    depth, half = own[0].shape[1:]

    def x_copy(i):
        return pltpu.make_async_copy(parts[i], x_all.at[:, pl.ds(i * depth, depth)], sems.at[i])

    def target(i, place):
        cols = pl.ds(pl.multiple_of(place * half, 128), half)
        return w_all.at[pl.ds(i * depth, depth), cols]

    for i in range(count):
        x_copy(i).start()
        for base, refs_of, place in ((32, own, core), (40, other, 1 - core)):
            start_block(table[base + first + i], refs_of, target(i, place), sems.at[i])

    total = None
    for lo in range(0, count, 2):
        hi = min(lo + 2, count)
        for i in range(lo, hi):
            x_copy(i).wait()
            for place in range(2):
                pltpu.make_async_copy(own[0].at[0], target(i, place), sems.at[i]).wait()
        span = slice(lo * depth, hi * depth)
        prod = jnp.dot(x_all[:, span], w_all[span, :], preferred_element_type=F32)
        total = prod if total is None else total + prod
    sum_copy.wait()
    out_ref[...] = (sum_all[...].astype(F32) + gate_ref[...] * total).astype(out_ref.dtype)


def output_rows(parts, first, own, other, table, so_far, gate, dtype):
    count = len(parts)
    rows, depth = parts[0].shape
    cols = 2 * own[0].shape[2]
    vmem = pl.BlockSpec(memory_space=pltpu.VMEM)
    anywhere = pl.BlockSpec(memory_space=pl.ANY)
    return pl.pallas_call(
        functools.partial(output_kernel, first, count),
        in_specs=[pl.BlockSpec(memory_space=pltpu.SMEM)] + [anywhere] * (count + 9) + [vmem],
        out_specs=vmem,
        out_shape=jax.ShapeDtypeStruct((rows, cols), dtype),
        scratch_shapes=[
            pltpu.VMEM((rows, count * depth), BF16),
            pltpu.VMEM((count * depth, cols), BF16),
            pltpu.VMEM((rows, cols), so_far.dtype),
            pltpu.SemaphoreType.DMA((count,)),
            pltpu.SemaphoreType.DMA,
        ],
        compiler_params=pltpu.CompilerParams(vmem_limit_bytes=VMEM_BYTES),
        name="output_rows",
    )(table, *parts, *own, *other, so_far, gate)


def stack_kernel(axis, *refs):
    blocks, out_ref, sems = refs[:-2], refs[-2], refs[-1]
    copies = []
    for i, block in enumerate(blocks):
        cols = block.shape[-1]
        target = out_ref.at[i] if axis == 0 else out_ref.at[:, pl.ds(i * cols, cols)]
        copies.append(pltpu.make_async_copy(block, target, sems.at[i]))
    for copy in copies:
        copy.start()
    for copy in copies:
        copy.wait()


def stack(blocks, axis=0):
    rows, cols = blocks[0].shape
    shape = (len(blocks), rows, cols) if axis == 0 else (rows, len(blocks) * cols)
    return pl.pallas_call(
        functools.partial(stack_kernel, axis),
        in_specs=[pl.BlockSpec(memory_space=pl.ANY)] * len(blocks),
        out_specs=pl.BlockSpec(memory_space=pltpu.VMEM),
        out_shape=jax.ShapeDtypeStruct(shape, blocks[0].dtype),
        scratch_shapes=[pltpu.SemaphoreType.DMA((len(blocks),))],
        name="stack",
    )(*blocks)


def places():
    rows = np.zeros((128, 48), np.int32)
    for tile in range(16):
        for hid in range(8):
            x, yl, yh, z, c = hid // 2, hid % 2, tile // 8, tile // 2 % 4, tile % 2
            row = rows[tile * 8 + hid]
            row[:8] = [(x + s) % 4 * 2 + (yl ^ k) for k in range(2) for s in (0, -way(c), way(c), 2)]
            row[16] = c
            for first, w in ((8, way(c)), (24, -way(c)), (32, way(c)), (40, -way(c))):
                pairs = [(yh ^ k) * 4 + (z + s) % 4 for k in range(2) for s in (0, -w, w, 2)]
                pairs = [pairs[i] for i in (0, 1, 2, 4, 5, 6, 3, 7)]
                if first >= 32:
                    pairs = [rows_held(hid, pair) for pair in pairs]
                row[first : first + 8] = [pairs.index(hid_of) for hid_of in row[:8]]
    return rows


def body(
    residual_in, w_query, w_key, w_value, w_output, shift_mod, scale_mod, gate_mod, neighbours
):
    tok_rows, feat_cols = residual_in.shape
    tile_id, hid_id = lax.axis_index("tile"), lax.axis_index("hid")
    table = lax.dynamic_index_in_dim(jnp.asarray(places()), tile_id * 8 + hid_id, 0, keepdims=False)

    listed = (neighbours >= 0).reshape(PER_LAYER, 3, 3, 3)
    grid = np.arange(PER_LAYER)
    row_step = grid[None, :] // PER_ROW - grid[:, None] // PER_ROW
    col_step = grid[None, :] % PER_ROW - grid[:, None] % PER_ROW
    bias = jnp.full((PER_LAYER, 3, PER_LAYER), -1e30, F32)
    for b in range(-1, 2):
        for e in range(-1, 2):
            here = jnp.asarray((row_step == b) & (col_step == e))[:, None, :]
            bias = jnp.where(here & listed[:, :, b + 1, e + 1][:, :, None], 0.0, bias)
    bias = jnp.repeat(bias.reshape(PER_LAYER, 3 * PER_LAYER), TILE, axis=1)

    gate = lax.dynamic_slice_in_dim(gate_mod, hid_id * feat_cols, feat_cols)[None]

    fence = lax.optimization_barrier
    weights = stack([w_key, w_value, w_query], axis=1)
    kv_cols = 2 * w_key.shape[1]
    w_rows, w_cols = weights.shape
    w_half = w_rows // 2
    x_a, x_b, w_a, w_b, w_mate, own, weights, bias, table, gate, o_block = fence(
        (
            send(residual_in, X_A),
            send(residual_in, X_B),
            send(weights, Z_A),
            send(weights, Z_B),
            send(weights, Y_HI),
            residual_in,
            weights,
            bias,
            table,
            gate,
            w_output,
        )
    )

    far, mate, w_mate_a, w_mate_b, o_block, x_a, x_b, w_a, w_b, own, w_mate, weights = fence(
        (
            send(own, X_2),
            send(own, Y_LO),
            send(w_mate, Z_A),
            send(w_mate, Z_B),
            send(o_block, SWAP_1),
            x_a,
            x_b,
            w_a,
            w_b,
            own,
            w_mate,
            weights,
        )
    )

    mate_a, mate_b, mate_far, w_fwd_a, w_fwd_b, early, o_block = fence(
        (
            send(mate, X_A),
            send(mate, X_B),
            send(far, Y_LO),
            send(jnp.stack([w_a[:w_half], w_mate_a[:w_half]]), Z_A),
            send(jnp.stack([w_b[w_half:], w_mate_b[w_half:]]), Z_B),
            stack([weights, w_a, w_b, w_mate, w_mate_a, w_mate_b]),
            o_block,
        )
    )

    mine = [early, w_fwd_a, w_fwd_b]
    x_other, first = modulate_project(
        [own, x_a, x_b, far, mate, mate_a, mate_b, mate_far],
        mine,
        table,
        scale_mod.reshape(8, 1, feat_cols),
        shift_mod.reshape(8, 1, feat_cols),
    )
    first, x_other, o_block, *theirs = fence(
        (first, x_other, send(o_block, SWAP_2), *[send(part, CORE) for part in mine])
    )

    key_value = project(x_other, theirs, table, 0, kv_cols, first)
    key_value, o_block, o_a, o_b, o_mate, first, x_other, *theirs = fence(
        (
            key_value,
            o_block,
            send(o_block, Z_A),
            send(o_block, Z_B),
            send(o_block, Y_HI),
            first,
            x_other,
            *theirs,
        )
    )

    queries = project(x_other, theirs, table, kv_cols, w_cols - kv_cols, first)
    before, later, queries, key_value, o_early, o_pair, o_mate = fence(
        (
            send(key_value, NEXT),
            send(key_value, PREV),
            queries,
            key_value,
            stack([o_block, o_a, o_b, o_mate]),
            stack([o_block, o_mate]),
            o_mate,
        )
    )

    pieces = attend(queries, before, key_value, later, bias)
    pieces, o_pair, o_mate_a, o_mate_b, o_early, o_early_other = fence(
        (
            pieces,
            o_pair,
            send(o_mate, Z_A),
            send(o_mate, Z_B),
            o_early,
            send(o_early, CORE),
        )
    )

    p_a, p_b, p_far, p_mate, pieces, o_ends, *o_others = fence(
        (
            send(pieces, X_A),
            send(pieces, X_B),
            send(pieces, X_2),
            send(pieces, Y_LO),
            pieces,
            send(o_pair, Z_2),
            send(o_mate_a, CORE),
            send(o_mate_b, CORE),
        )
    )
    o_mine = [o_early, o_mate_a, o_mate_b, o_ends]
    o_theirs = [o_early_other, *o_others, send(o_ends, CORE)]
    p_mate_a = send(p_mate, X_A)
    p_mate_b = send(p_mate, X_B)
    p_mate_far = send(p_far, Y_LO)
    near = [pieces, p_a, p_b, p_far, p_mate]
    near = output_rows(near, 0, o_mine, o_theirs, table, residual_in, gate, F32)
    ends = [p_mate_a, p_mate_b, p_mate_far]
    return output_rows(ends, 5, o_mine, o_theirs, table, near, gate, BF16)


def solution(mesh):
    placed = (
        P("tile", "hid"),
        P("tile", "hid"),
        P("tile", "hid"),
        P("tile", "hid"),
        P("hid", "tile"),
        P(),
        P(),
        P(),
        P("tile", None),
    )
    return jax.shard_map(
        body, mesh=mesh, in_specs=placed, out_specs=P("tile", "hid"), check_vma=False
    )
```

```python
import functools

import jax
import jax.numpy as jnp
import numpy as np
from jax import lax
from jax.experimental import pallas as pl
from jax.experimental.pallas import tpu as pltpu
from jax.sharding import PartitionSpec as P

HD = 128
TILE = 32
PER_ROW = 4
PER_LAYER = 16
LAYER = PER_LAYER * TILE
AXES = ("tile", "hid")
F32 = jnp.float32
BF16 = jnp.bfloat16


def route(move):
    pairs = []
    for x in range(4):
        for yl in range(2):
            for yh in range(2):
                for z in range(4):
                    for c in range(2):
                        a, b, d, e, f = move(x, yl, yh, z, c)
                        source = (yh * 8 + z * 2 + c) * 8 + x * 2 + yl
                        target = (d * 8 + e % 4 * 2 + f) * 8 + a % 4 * 2 + b
                        pairs.append((source, target))
    return pairs


def way(c):
    return 1 - 2 * c


X_A = route(lambda x, yl, yh, z, c: (x + way(c), yl, yh, z, c))
X_B = route(lambda x, yl, yh, z, c: (x - way(c), yl, yh, z, c))
X_1 = route(lambda x, yl, yh, z, c: (x ^ 1, yl, yh, z, c))
X_2 = route(lambda x, yl, yh, z, c: (x + 2, yl, yh, z, c))
Z_A = route(lambda x, yl, yh, z, c: (x, yl, yh, z + way(c), c))
Z_2 = route(lambda x, yl, yh, z, c: (x, yl, yh, z + 2, c))
Z_B = route(lambda x, yl, yh, z, c: (x, yl, yh, z - way(c), c))
Y_LO = route(lambda x, yl, yh, z, c: (x, 1 - yl, yh, z, c))
Y_HI = route(lambda x, yl, yh, z, c: (x, yl, 1 - yh, z, c))
CORE = route(lambda x, yl, yh, z, c: (x, yl, yh, z, 1 - c))
SWAP_1 = route(lambda x, yl, yh, z, c: (x, yl, yh ^ x // 2, z + 2 * (x % 2) + yl, c))


def second_move(x, yl, yh, z, c):
    from_z = (z - 2 * (x % 2) - yl) % 4
    return 2 * (yh ^ x // 2) + from_z // 2, from_z % 2, yh, z, c


SWAP_2 = route(second_move)


def rows_held(hid, pair):
    return (pair // 4 ^ hid // 4) * 4 + (pair - hid) % 4


NEXT = [(t * 8 + h, t * 8 + 8 + h) for t in range(15) for h in range(8)]
PREV = [(t * 8 + 8 + h, t * 8 + h) for t in range(15) for h in range(8)]


def send(array, pairs):
    return lax.ppermute(array, AXES, pairs)


def after(array, *others):
    return lax.optimization_barrier((array, *others))[0]


VMEM_BYTES = 60 * 2**20


def place_copies(place, parts, target, sem):
    first = 0
    for part in parts:
        count = part.shape[0] if len(part.shape) == 3 else 1
        source = part.at[jnp.clip(place - first, 0, count - 1)] if len(part.shape) == 3 else part
        here = (place >= first) & (place < first + count)
        yield here, pltpu.make_async_copy(source, target, sem)
        first += count


def start_block(place, parts, target, sem):
    for here, copy in place_copies(place, parts, target, sem):

        @pl.when(here)
        def _():
            copy.start()


def modulate_project_kernel(table, *refs):
    blocks, parts, refs = refs[:8], refs[8:11], refs[11:]
    gain_ref, move_ref, other_out, out_ref, raw, own, other, w_all, x_sems, w_sems, out_sem = refs
    rows, depth = blocks[0].shape
    half = depth // 2
    for i in range(8):
        pltpu.make_async_copy(blocks[i], raw.at[i], x_sems.at[i]).start()

    def fold(value):
        return sum(value[:, lane : lane + 128] for lane in range(0, depth, 128))

    total = jnp.zeros((rows, 128), F32)
    for i in range(8):
        pltpu.make_async_copy(blocks[i], raw.at[i], x_sems.at[i]).wait()
        total += fold(raw[i].astype(F32))
    for i in range(8):
        start_block(table[8 + i], parts, w_all.at[pl.ds(i * half, half), :], w_sems.at[i])
    centre = jnp.sum(total, axis=1, keepdims=True) / (8 * depth)
    spread = jnp.zeros((rows, 128), F32)
    for i in range(8):
        spread += fold(jnp.square(raw[i].astype(F32) - centre))
    scale = lax.rsqrt(jnp.sum(spread, axis=1, keepdims=True) / (8 * depth) + 1e-06)

    def modulate(low_ref, high_ref):
        for i in range(8):
            value = (raw[i].astype(F32) - centre) * scale
            value = (value * (1.0 + gain_ref[table[i]]) + move_ref[table[i]]).astype(BF16)
            low_ref[:, i * half : (i + 1) * half] = value[:, :half]
            high_ref[:, i * half : (i + 1) * half] = value[:, half:]

    @pl.when(table[16] == 0)
    def _():
        modulate(own, other)

    @pl.when(table[16] == 1)
    def _():
        modulate(other, own)

    copy = pltpu.make_async_copy(other, other_out, out_sem)
    copy.start()
    for i in range(8):
        target = w_all.at[pl.ds(i * half, half), :]
        pltpu.make_async_copy(parts[0].at[0], target, w_sems.at[i]).wait()
    out_ref[...] = jnp.dot(own[...], w_all[...], preferred_element_type=F32)
    copy.wait()


def modulate_project(blocks, weights, table, gains, moves):
    rows, depth = blocks[0].shape
    cols = weights[0].shape[2]
    half = (rows, 4 * depth)
    vmem = pl.BlockSpec(memory_space=pltpu.VMEM)
    anywhere = pl.BlockSpec(memory_space=pl.ANY)
    return pl.pallas_call(
        modulate_project_kernel,
        in_specs=[pl.BlockSpec(memory_space=pltpu.SMEM)] + [anywhere] * 11 + [vmem] * 2,
        out_specs=[anywhere, vmem],
        out_shape=[jax.ShapeDtypeStruct(half, BF16), jax.ShapeDtypeStruct((rows, cols), F32)],
        scratch_shapes=[
            pltpu.VMEM((8, rows, depth), BF16),
            pltpu.VMEM(half, BF16),
            pltpu.VMEM(half, BF16),
            pltpu.VMEM((4 * depth, cols), BF16),
            pltpu.SemaphoreType.DMA((8,)),
            pltpu.SemaphoreType.DMA((8,)),
            pltpu.SemaphoreType.DMA,
        ],
        compiler_params=pltpu.CompilerParams(vmem_limit_bytes=VMEM_BYTES),
        name="modulate_project",
    )(table, *blocks, *weights, gains, moves)


def project_kernel(first_col, table, x_ref, *refs):
    parts, (add_ref, out_ref, x_all, w_all, sum_all, x_sems, w_sems, sum_sem) = refs[:3], refs[3:]
    depth = x_ref.shape[1] // 8
    cols = out_ref.shape[1]
    span = pl.ds(first_col, cols)
    parts = [parts[0].at[:, :, span], parts[1].at[:, span], parts[2].at[:, span]]
    pieces = (0, 2, 5, 8)

    def x_copy(n):
        lo, hi = pieces[n], pieces[n + 1]
        here = pl.ds(lo * depth, (hi - lo) * depth)
        return pltpu.make_async_copy(x_ref.at[:, here], x_all.at[:, here], x_sems.at[n])

    def target(i):
        return w_all.at[pl.ds(i * depth, depth), :]

    def start(n):
        x_copy(n).start()
        for i in range(pieces[n], pieces[n + 1]):
            start_block(table[24 + i], parts, target(i), w_sems.at[i])

    sum_copy = pltpu.make_async_copy(add_ref.at[:, span], sum_all, sum_sem)
    start(0)
    start(1)
    total = None
    for n in range(3):
        x_copy(n).wait()
        for i in range(pieces[n], pieces[n + 1]):
            pltpu.make_async_copy(parts[0].at[0], target(i), w_sems.at[i]).wait()
        if n == 0:
            start(2)
            sum_copy.start()
        here = slice(pieces[n] * depth, pieces[n + 1] * depth)
        prod = jnp.dot(x_all[:, here], w_all[here, :], preferred_element_type=F32)
        total = prod if total is None else total + prod
    sum_copy.wait()
    out_ref[...] = (total + sum_all[...]).astype(BF16)


def project(x, weights, table, first_col, cols, add):
    rows, width = x.shape
    return pl.pallas_call(
        functools.partial(project_kernel, first_col),
        in_specs=[pl.BlockSpec(memory_space=pltpu.SMEM)] + [pl.BlockSpec(memory_space=pl.ANY)] * 5,
        out_specs=pl.BlockSpec(memory_space=pltpu.VMEM),
        out_shape=jax.ShapeDtypeStruct((rows, cols), BF16),
        scratch_shapes=[
            pltpu.VMEM((rows, width), BF16),
            pltpu.VMEM((width, cols), BF16),
            pltpu.VMEM((rows, cols), F32),
            pltpu.SemaphoreType.DMA((3,)),
            pltpu.SemaphoreType.DMA((8,)),
            pltpu.SemaphoreType.DMA,
        ],
        compiler_params=pltpu.CompilerParams(vmem_limit_bytes=VMEM_BYTES),
        name="project",
    )(table, x, *weights, add)


def attend_kernel(heads, *refs):
    sources, (out_ref, q_ref, prev_ref, own_ref, next_ref, bias_ref, sems) = refs[:5], refs[5:]
    copies = [
        pltpu.make_async_copy(source, target, sems.at[i])
        for i, (source, target) in enumerate(zip(sources, (q_ref, prev_ref, own_ref, next_ref, bias_ref)))
    ]
    for copy in copies:
        copy.start()
    for copy in copies:
        copy.wait()
    width = heads * HD
    row_len = PER_ROW * TILE
    for head in range(heads):
        cols = slice(head * HD, (head + 1) * HD)
        v_cols = slice(width + head * HD, width + (head + 1) * HD)
        for row in range(PER_LAYER // PER_ROW):
            lo = max(row - 1, 0) * row_len
            hi = min(row + 2, PER_LAYER // PER_ROW) * row_len
            queries = q_ref[row * row_len : (row + 1) * row_len, cols]
            scores = []
            for block, ref in enumerate((prev_ref, own_ref, next_ref)):
                part = lax.dot_general(
                    queries,
                    ref[lo:hi, cols],
                    (((1,), (1,)), ((), ())),
                    preferred_element_type=F32,
                ) * HD ** (-0.5)
                tiles = bias_ref[row * PER_ROW : (row + 1) * PER_ROW, block * LAYER + lo : block * LAYER + hi]
                part = part.reshape(PER_ROW, TILE, hi - lo) + tiles[:, None, :]
                scores.append(part.reshape(row_len, hi - lo))
            peak = functools.reduce(
                jnp.maximum, [jnp.max(part, axis=1, keepdims=True) for part in scores]
            )
            chances = [jnp.exp(part - peak) for part in scores]
            denom = sum(jnp.sum(part, axis=1, keepdims=True) for part in chances)
            total = sum(
                jnp.dot(part.astype(BF16), ref[lo:hi, v_cols], preferred_element_type=F32)
                for part, ref in zip(chances, (prev_ref, own_ref, next_ref))
            )
            out_ref[row * row_len : (row + 1) * row_len, cols] = (total / denom).astype(BF16)


def attend(*arrays):
    queries = arrays[0]
    heads = queries.shape[1] // HD
    return pl.pallas_call(
        functools.partial(attend_kernel, heads),
        in_specs=[pl.BlockSpec(memory_space=pl.ANY)] * 5,
        out_specs=pl.BlockSpec(memory_space=pltpu.VMEM),
        out_shape=jax.ShapeDtypeStruct(queries.shape, BF16),
        scratch_shapes=[pltpu.VMEM(array.shape, array.dtype) for array in arrays]
        + [pltpu.SemaphoreType.DMA((5,))],
        compiler_params=pltpu.CompilerParams(vmem_limit_bytes=40 * 2**20),
        name="attend",
    )(*arrays)


def output_kernel(first, count, table, *refs):
    parts, own, other = refs[:count], refs[count : count + 5], refs[count + 5 : count + 10]
    sum_ref, gate_ref, out_ref, x_all, w_all, sum_all, sems, sum_sem = refs[count + 10 :]
    sum_copy = pltpu.make_async_copy(sum_ref, sum_all, sum_sem)
    sum_copy.start()
    core = table[16]
    depth, half = own[0].shape[1:]

    def x_copy(i):
        return pltpu.make_async_copy(parts[i], x_all.at[:, pl.ds(i * depth, depth)], sems.at[i])

    def target(i, place):
        cols = pl.ds(pl.multiple_of(place * half, 128), half)
        return w_all.at[pl.ds(i * depth, depth), cols]

    for i in range(count):
        x_copy(i).start()
        for base, refs_of, place in ((32, own, core), (40, other, 1 - core)):
            start_block(table[base + first + i], refs_of, target(i, place), sems.at[i])

    total = None
    for lo in range(0, count, 2):
        hi = min(lo + 2, count)
        for i in range(lo, hi):
            x_copy(i).wait()
            for place in range(2):
                pltpu.make_async_copy(own[0].at[0], target(i, place), sems.at[i]).wait()
        span = slice(lo * depth, hi * depth)
        prod = jnp.dot(x_all[:, span], w_all[span, :], preferred_element_type=F32)
        total = prod if total is None else total + prod
    sum_copy.wait()
    out_ref[...] = (sum_all[...].astype(F32) + gate_ref[...] * total).astype(out_ref.dtype)


def output_rows(parts, first, own, other, table, so_far, gate, dtype):
    count = len(parts)
    rows, depth = parts[0].shape
    cols = 2 * own[0].shape[2]
    vmem = pl.BlockSpec(memory_space=pltpu.VMEM)
    anywhere = pl.BlockSpec(memory_space=pl.ANY)
    return pl.pallas_call(
        functools.partial(output_kernel, first, count),
        in_specs=[pl.BlockSpec(memory_space=pltpu.SMEM)] + [anywhere] * (count + 11) + [vmem],
        out_specs=vmem,
        out_shape=jax.ShapeDtypeStruct((rows, cols), dtype),
        scratch_shapes=[
            pltpu.VMEM((rows, count * depth), BF16),
            pltpu.VMEM((count * depth, cols), BF16),
            pltpu.VMEM((rows, cols), so_far.dtype),
            pltpu.SemaphoreType.DMA((count,)),
            pltpu.SemaphoreType.DMA,
        ],
        compiler_params=pltpu.CompilerParams(vmem_limit_bytes=40 * 2**20),
        name="output_rows",
    )(table, *parts, *own, *other, so_far, gate)


def stack_kernel(axis, *refs):
    blocks, out_ref, sems = refs[:-2], refs[-2], refs[-1]
    copies = []
    for i, block in enumerate(blocks):
        cols = block.shape[-1]
        target = out_ref.at[i] if axis == 0 else out_ref.at[:, pl.ds(i * cols, cols)]
        copies.append(pltpu.make_async_copy(block, target, sems.at[i]))
    for copy in copies:
        copy.start()
    for copy in copies:
        copy.wait()


def stack(blocks, axis=0):
    rows, cols = blocks[0].shape
    shape = (len(blocks), rows, cols) if axis == 0 else (rows, len(blocks) * cols)
    return pl.pallas_call(
        functools.partial(stack_kernel, axis),
        in_specs=[pl.BlockSpec(memory_space=pl.ANY)] * len(blocks),
        out_specs=pl.BlockSpec(memory_space=pltpu.VMEM),
        out_shape=jax.ShapeDtypeStruct(shape, blocks[0].dtype),
        scratch_shapes=[pltpu.SemaphoreType.DMA((len(blocks),))],
        name="stack",
    )(*blocks)


def places():
    rows = np.zeros((128, 48), np.int32)
    for tile in range(16):
        for hid in range(8):
            x, yl, yh, z, c = hid // 2, hid % 2, tile // 8, tile // 2 % 4, tile % 2
            row = rows[tile * 8 + hid]
            row[:8] = [(x + s) % 4 * 2 + (yl ^ k) for k in range(2) for s in (0, -way(c), way(c), 2)]
            row[16] = c
            for first, w in ((8, way(c)), (24, -way(c)), (32, way(c)), (40, -way(c))):
                pairs = [(yh ^ k) * 4 + (z + s) % 4 for k in range(2) for s in (0, -w, w, 2)]
                pairs = [pairs[i] for i in (0, 1, 2, 4, 5, 6, 3, 7)]
                if first >= 32:
                    pairs = [rows_held(hid, pair) for pair in pairs]
                row[first : first + 8] = [pairs.index(hid_of) for hid_of in row[:8]]
    return rows


def body(
    residual_in, w_query, w_key, w_value, w_output, shift_mod, scale_mod, gate_mod, neighbours
):
    tok_rows, feat_cols = residual_in.shape
    tile_id, hid_id = lax.axis_index("tile"), lax.axis_index("hid")
    table = lax.dynamic_index_in_dim(jnp.asarray(places()), tile_id * 8 + hid_id, 0, keepdims=False)

    listed = (neighbours >= 0).reshape(PER_LAYER, 3, 3, 3)
    grid = np.arange(PER_LAYER)
    row_step = grid[None, :] // PER_ROW - grid[:, None] // PER_ROW
    col_step = grid[None, :] % PER_ROW - grid[:, None] % PER_ROW
    bias = jnp.full((PER_LAYER, 3, PER_LAYER), -1e30, F32)
    for b in range(-1, 2):
        for e in range(-1, 2):
            here = jnp.asarray((row_step == b) & (col_step == e))[:, None, :]
            bias = jnp.where(here & listed[:, :, b + 1, e + 1][:, :, None], 0.0, bias)
    bias = jnp.repeat(bias.reshape(PER_LAYER, 3 * PER_LAYER), TILE, axis=1)

    gate = lax.dynamic_slice_in_dim(gate_mod, hid_id * feat_cols, feat_cols)[None]

    fence = lax.optimization_barrier
    weights = stack([w_key, w_value, w_query], axis=1)
    kv_cols = 2 * w_key.shape[1]
    w_cols = weights.shape[1]
    x_a, x_b, w_a, w_b, w_mate, own, weights, bias, table, gate, o_block = fence(
        (
            send(residual_in, X_A),
            send(residual_in, X_B),
            send(weights, Z_A),
            send(weights, Z_B),
            send(weights, Y_HI),
            residual_in,
            weights,
            bias,
            table,
            gate,
            w_output,
        )
    )

    far, mate, w_mate_a, w_mate_b, o_block, x_a, x_b, w_a, w_b, own, w_mate, weights = fence(
        (
            send(own, X_2),
            send(own, Y_LO),
            send(w_mate, Z_A),
            send(w_mate, Z_B),
            send(o_block, SWAP_1),
            x_a,
            x_b,
            w_a,
            w_b,
            own,
            w_mate,
            weights,
        )
    )

    mate_a, mate_b, mate_far, w_far, w_mate_far, early, o_block = fence(
        (
            send(mate, X_A),
            send(mate, X_B),
            send(far, Y_LO),
            send(w_a, Z_A),
            send(w_mate_b, Z_B),
            stack([weights, w_a, w_b, w_mate, w_mate_a, w_mate_b]),
            o_block,
        )
    )

    mine = [early, w_far, w_mate_far]
    x_other, first = modulate_project(
        [own, x_a, x_b, far, mate, mate_a, mate_b, mate_far],
        mine,
        table,
        scale_mod.reshape(8, 1, feat_cols),
        shift_mod.reshape(8, 1, feat_cols),
    )
    first, x_other, o_block, *theirs = fence(
        (first, x_other, send(o_block, SWAP_2), *[send(part, CORE) for part in mine])
    )

    key_value = project(x_other, theirs, table, 0, kv_cols, first)
    key_value, o_block, o_a, o_b, o_mate, first, x_other, *theirs = fence(
        (
            key_value,
            o_block,
            send(o_block, Z_A),
            send(o_block, Z_B),
            send(o_block, Y_HI),
            first,
            x_other,
            *theirs,
        )
    )

    queries = project(x_other, theirs, table, kv_cols, w_cols - kv_cols, first)
    before, later, queries, key_value, o_early, o_a, o_mate = fence(
        (
            send(key_value, NEXT),
            send(key_value, PREV),
            queries,
            key_value,
            stack([o_block, o_a, o_b, o_mate]),
            o_a,
            o_mate,
        )
    )

    pieces = attend(queries, before, key_value, later, bias)
    pieces, o_mate_a, o_mate_b, o_a, o_early, o_early_other = fence(
        (
            pieces,
            send(o_mate, Z_A),
            send(o_mate, Z_B),
            o_a,
            o_early,
            send(o_early, CORE),
        )
    )

    p_a, p_b, p_far, p_mate, pieces, *o_rest = fence(
        (
            send(pieces, X_A),
            send(pieces, X_B),
            send(pieces, X_2),
            send(pieces, Y_LO),
            pieces,
            send(o_a, Z_A),
            send(o_mate_b, Z_B),
            send(o_mate_a, CORE),
            send(o_mate_b, CORE),
        )
    )
    o_ends, o_others = o_rest[:2], o_rest[2:]
    o_mine = [o_early, o_mate_a, o_mate_b, *o_ends]
    o_theirs = [o_early_other, *o_others, *[send(part, CORE) for part in o_ends]]
    p_mate_a = send(p_mate, X_A)
    p_mate_b = send(p_mate, X_B)
    p_mate_far = send(p_far, Y_LO)
    near = [pieces, p_a, p_b, p_far, p_mate]
    near = output_rows(near, 0, o_mine, o_theirs, table, residual_in, gate, F32)
    ends = [p_mate_a, p_mate_b, p_mate_far]
    return output_rows(ends, 5, o_mine, o_theirs, table, near, gate, BF16)


def solution(mesh):
    placed = (
        P("tile", "hid"),
        P("tile", "hid"),
        P("tile", "hid"),
        P("tile", "hid"),
        P("hid", "tile"),
        P(),
        P(),
        P(),
        P("tile", None),
    )
    return jax.shard_map(
        body, mesh=mesh, in_specs=placed, out_specs=P("tile", "hid"), check_vma=False
    )
```

```python
import functools

import jax
import jax.numpy as jnp
import numpy as np
from jax import lax
from jax.experimental import pallas as pl
from jax.experimental.pallas import tpu as pltpu
from jax.sharding import PartitionSpec as P

HD = 128
TILE = 32
PER_ROW = 4
PER_LAYER = 16
LAYER = PER_LAYER * TILE
AXES = ("tile", "hid")
F32 = jnp.float32
BF16 = jnp.bfloat16


def route(move):
    pairs = []
    for x in range(4):
        for yl in range(2):
            for yh in range(2):
                for z in range(4):
                    for c in range(2):
                        a, b, d, e, f = move(x, yl, yh, z, c)
                        source = (yh * 8 + z * 2 + c) * 8 + x * 2 + yl
                        target = (d * 8 + e % 4 * 2 + f) * 8 + a % 4 * 2 + b
                        pairs.append((source, target))
    return pairs


def way(c):
    return 1 - 2 * c


X_A = route(lambda x, yl, yh, z, c: (x + way(c), yl, yh, z, c))
X_B = route(lambda x, yl, yh, z, c: (x - way(c), yl, yh, z, c))
X_1 = route(lambda x, yl, yh, z, c: (x ^ 1, yl, yh, z, c))
X_2 = route(lambda x, yl, yh, z, c: (x + 2, yl, yh, z, c))
Z_A = route(lambda x, yl, yh, z, c: (x, yl, yh, z + way(c), c))
Z_2 = route(lambda x, yl, yh, z, c: (x, yl, yh, z + 2, c))
Z_B = route(lambda x, yl, yh, z, c: (x, yl, yh, z - way(c), c))
Y_LO = route(lambda x, yl, yh, z, c: (x, 1 - yl, yh, z, c))
Y_HI = route(lambda x, yl, yh, z, c: (x, yl, 1 - yh, z, c))
CORE = route(lambda x, yl, yh, z, c: (x, yl, yh, z, 1 - c))
SWAP_1 = route(lambda x, yl, yh, z, c: (x, yl, yh ^ x // 2, z + 2 * (x % 2) + yl, c))


def second_move(x, yl, yh, z, c):
    from_z = (z - 2 * (x % 2) - yl) % 4
    return 2 * (yh ^ x // 2) + from_z // 2, from_z % 2, yh, z, c


SWAP_2 = route(second_move)


def rows_held(hid, pair):
    return (pair // 4 ^ hid // 4) * 4 + (pair - hid) % 4


NEXT = [(t * 8 + h, t * 8 + 8 + h) for t in range(15) for h in range(8)]
PREV = [(t * 8 + 8 + h, t * 8 + h) for t in range(15) for h in range(8)]


def send(array, pairs):
    return lax.ppermute(array, AXES, pairs)


def after(array, *others):
    return lax.optimization_barrier((array, *others))[0]


VMEM_BYTES = 60 * 2**20


def place_copies(place, parts, target, sem):
    first = 0
    for part in parts:
        count = part.shape[0] if len(part.shape) == 3 else 1
        source = part.at[jnp.clip(place - first, 0, count - 1)] if len(part.shape) == 3 else part
        here = (place >= first) & (place < first + count)
        yield here, pltpu.make_async_copy(source, target, sem)
        first += count


def start_block(place, parts, target, sem):
    for here, copy in place_copies(place, parts, target, sem):

        @pl.when(here)
        def _():
            copy.start()


def modulate_project_kernel(table, *refs):
    blocks, parts, refs = refs[:8], refs[8:11], refs[11:]
    gain_ref, move_ref, other_out, out_ref, raw, own, other, w_all, x_sems, w_sems, out_sem = refs
    rows, depth = blocks[0].shape
    half = depth // 2
    for i in range(8):
        pltpu.make_async_copy(blocks[i], raw.at[i], x_sems.at[i]).start()

    def fold(value):
        return sum(value[:, lane : lane + 128] for lane in range(0, depth, 128))

    total = jnp.zeros((rows, 128), F32)
    for i in range(8):
        pltpu.make_async_copy(blocks[i], raw.at[i], x_sems.at[i]).wait()
        total += fold(raw[i].astype(F32))
    for i in range(8):
        start_block(table[8 + i], parts, w_all.at[pl.ds(i * half, half), :], w_sems.at[i])
    centre = jnp.sum(total, axis=1, keepdims=True) / (8 * depth)
    spread = jnp.zeros((rows, 128), F32)
    for i in range(8):
        spread += fold(jnp.square(raw[i].astype(F32) - centre))
    scale = lax.rsqrt(jnp.sum(spread, axis=1, keepdims=True) / (8 * depth) + 1e-06)

    def modulate(low_ref, high_ref):
        for i in range(8):
            value = (raw[i].astype(F32) - centre) * scale
            value = (value * (1.0 + gain_ref[table[i]]) + move_ref[table[i]]).astype(BF16)
            low_ref[:, i * half : (i + 1) * half] = value[:, :half]
            high_ref[:, i * half : (i + 1) * half] = value[:, half:]

    @pl.when(table[16] == 0)
    def _():
        modulate(own, other)

    @pl.when(table[16] == 1)
    def _():
        modulate(other, own)

    copy = pltpu.make_async_copy(other, other_out, out_sem)
    copy.start()
    for i in range(8):
        target = w_all.at[pl.ds(i * half, half), :]
        pltpu.make_async_copy(parts[0].at[0], target, w_sems.at[i]).wait()
    out_ref[...] = jnp.dot(own[...], w_all[...], preferred_element_type=F32)
    copy.wait()


def modulate_project(blocks, weights, table, gains, moves):
    rows, depth = blocks[0].shape
    cols = weights[0].shape[2]
    half = (rows, 4 * depth)
    vmem = pl.BlockSpec(memory_space=pltpu.VMEM)
    anywhere = pl.BlockSpec(memory_space=pl.ANY)
    return pl.pallas_call(
        modulate_project_kernel,
        in_specs=[pl.BlockSpec(memory_space=pltpu.SMEM)] + [anywhere] * 11 + [vmem] * 2,
        out_specs=[anywhere, vmem],
        out_shape=[jax.ShapeDtypeStruct(half, BF16), jax.ShapeDtypeStruct((rows, cols), F32)],
        scratch_shapes=[
            pltpu.VMEM((8, rows, depth), BF16),
            pltpu.VMEM(half, BF16),
            pltpu.VMEM(half, BF16),
            pltpu.VMEM((4 * depth, cols), BF16),
            pltpu.SemaphoreType.DMA((8,)),
            pltpu.SemaphoreType.DMA((8,)),
            pltpu.SemaphoreType.DMA,
        ],
        compiler_params=pltpu.CompilerParams(vmem_limit_bytes=VMEM_BYTES),
        name="modulate_project",
    )(table, *blocks, *weights, gains, moves)


def project_kernel(first_col, table, x_ref, *refs):
    parts, (add_ref, out_ref, x_all, w_all, sum_all, x_sems, w_sems, sum_sem) = refs[:3], refs[3:]
    depth = x_ref.shape[1] // 8
    cols = out_ref.shape[1]
    span = pl.ds(first_col, cols)
    parts = [parts[0].at[:, :, span], parts[1].at[:, span], parts[2].at[:, span]]
    pieces = (0, 2, 5, 8)

    def x_copy(n):
        lo, hi = pieces[n], pieces[n + 1]
        here = pl.ds(lo * depth, (hi - lo) * depth)
        return pltpu.make_async_copy(x_ref.at[:, here], x_all.at[:, here], x_sems.at[n])

    def target(i):
        return w_all.at[pl.ds(i * depth, depth), :]

    def start(n):
        x_copy(n).start()
        for i in range(pieces[n], pieces[n + 1]):
            start_block(table[24 + i], parts, target(i), w_sems.at[i])

    sum_copy = pltpu.make_async_copy(add_ref.at[:, span], sum_all, sum_sem)
    start(0)
    start(1)
    total = None
    for n in range(3):
        x_copy(n).wait()
        for i in range(pieces[n], pieces[n + 1]):
            pltpu.make_async_copy(parts[0].at[0], target(i), w_sems.at[i]).wait()
        if n == 0:
            start(2)
            sum_copy.start()
        here = slice(pieces[n] * depth, pieces[n + 1] * depth)
        prod = jnp.dot(x_all[:, here], w_all[here, :], preferred_element_type=F32)
        total = prod if total is None else total + prod
    sum_copy.wait()
    out_ref[...] = (total + sum_all[...]).astype(BF16)


def project(x, weights, table, first_col, cols, add):
    rows, width = x.shape
    return pl.pallas_call(
        functools.partial(project_kernel, first_col),
        in_specs=[pl.BlockSpec(memory_space=pltpu.SMEM)] + [pl.BlockSpec(memory_space=pl.ANY)] * 5,
        out_specs=pl.BlockSpec(memory_space=pltpu.VMEM),
        out_shape=jax.ShapeDtypeStruct((rows, cols), BF16),
        scratch_shapes=[
            pltpu.VMEM((rows, width), BF16),
            pltpu.VMEM((width, cols), BF16),
            pltpu.VMEM((rows, cols), F32),
            pltpu.SemaphoreType.DMA((3,)),
            pltpu.SemaphoreType.DMA((8,)),
            pltpu.SemaphoreType.DMA,
        ],
        compiler_params=pltpu.CompilerParams(vmem_limit_bytes=VMEM_BYTES),
        name="project",
    )(table, x, *weights, add)


def attend_kernel(heads, *refs):
    sources, (out_ref, q_ref, prev_ref, own_ref, next_ref, bias_ref, sems) = refs[:5], refs[5:]
    copies = [
        pltpu.make_async_copy(source, target, sems.at[i])
        for i, (source, target) in enumerate(zip(sources, (q_ref, prev_ref, own_ref, next_ref, bias_ref)))
    ]
    for copy in copies:
        copy.start()
    for copy in copies:
        copy.wait()
    width = heads * HD
    row_len = PER_ROW * TILE
    for head in range(heads):
        cols = slice(head * HD, (head + 1) * HD)
        v_cols = slice(width + head * HD, width + (head + 1) * HD)
        for row in range(PER_LAYER // PER_ROW):
            lo = max(row - 1, 0) * row_len
            hi = min(row + 2, PER_LAYER // PER_ROW) * row_len
            queries = q_ref[row * row_len : (row + 1) * row_len, cols]
            scores = []
            for block, ref in enumerate((prev_ref, own_ref, next_ref)):
                part = lax.dot_general(
                    queries,
                    ref[lo:hi, cols],
                    (((1,), (1,)), ((), ())),
                    preferred_element_type=F32,
                ) * HD ** (-0.5)
                tiles = bias_ref[row * PER_ROW : (row + 1) * PER_ROW, block * LAYER + lo : block * LAYER + hi]
                part = part.reshape(PER_ROW, TILE, hi - lo) + tiles[:, None, :]
                scores.append(part.reshape(row_len, hi - lo))
            peak = functools.reduce(
                jnp.maximum, [jnp.max(part, axis=1, keepdims=True) for part in scores]
            )
            chances = [jnp.exp(part - peak) for part in scores]
            denom = sum(jnp.sum(part, axis=1, keepdims=True) for part in chances)
            total = sum(
                jnp.dot(part.astype(BF16), ref[lo:hi, v_cols], preferred_element_type=F32)
                for part, ref in zip(chances, (prev_ref, own_ref, next_ref))
            )
            out_ref[row * row_len : (row + 1) * row_len, cols] = (total / denom).astype(BF16)


def attend(*arrays):
    queries = arrays[0]
    heads = queries.shape[1] // HD
    return pl.pallas_call(
        functools.partial(attend_kernel, heads),
        in_specs=[pl.BlockSpec(memory_space=pl.ANY)] * 5,
        out_specs=pl.BlockSpec(memory_space=pltpu.VMEM),
        out_shape=jax.ShapeDtypeStruct(queries.shape, BF16),
        scratch_shapes=[pltpu.VMEM(array.shape, array.dtype) for array in arrays]
        + [pltpu.SemaphoreType.DMA((5,))],
        compiler_params=pltpu.CompilerParams(vmem_limit_bytes=40 * 2**20),
        name="attend",
    )(*arrays)


def output_kernel(first, count, table, *refs):
    parts, own, other = refs[:count], refs[count : count + 8], refs[count + 8 : count + 16]
    sum_ref, gate_ref, out_ref, x_all, w_all, sum_all, sems, sum_sem = refs[count + 16 :]
    sum_copy = pltpu.make_async_copy(sum_ref, sum_all, sum_sem)
    sum_copy.start()
    core = table[16]
    depth, half = own[0].shape

    def x_copy(i):
        return pltpu.make_async_copy(parts[i], x_all.at[:, pl.ds(i * depth, depth)], sems.at[i])

    def target(i, place):
        cols = pl.ds(pl.multiple_of(place * half, 128), half)
        return w_all.at[pl.ds(i * depth, depth), cols]

    for i in range(count):
        x_copy(i).start()
        for base, refs_of, place in ((32, own, core), (40, other, 1 - core)):
            start_block(table[base + first + i], refs_of, target(i, place), sems.at[i])

    total = None
    for lo in range(0, count, 2):
        hi = min(lo + 2, count)
        for i in range(lo, hi):
            x_copy(i).wait()
            for place in range(2):
                pltpu.make_async_copy(own[0], target(i, place), sems.at[i]).wait()
        span = slice(lo * depth, hi * depth)
        prod = jnp.dot(x_all[:, span], w_all[span, :], preferred_element_type=F32)
        total = prod if total is None else total + prod
    sum_copy.wait()
    out_ref[...] = (sum_all[...].astype(F32) + gate_ref[...] * total).astype(out_ref.dtype)


def output_rows(parts, first, own, other, table, so_far, gate, dtype):
    count = len(parts)
    rows, depth = parts[0].shape
    cols = 2 * own[0].shape[1]
    vmem = pl.BlockSpec(memory_space=pltpu.VMEM)
    anywhere = pl.BlockSpec(memory_space=pl.ANY)
    return pl.pallas_call(
        functools.partial(output_kernel, first, count),
        in_specs=[pl.BlockSpec(memory_space=pltpu.SMEM)] + [anywhere] * (count + 17) + [vmem],
        out_specs=vmem,
        out_shape=jax.ShapeDtypeStruct((rows, cols), dtype),
        scratch_shapes=[
            pltpu.VMEM((rows, count * depth), BF16),
            pltpu.VMEM((count * depth, cols), BF16),
            pltpu.VMEM((rows, cols), so_far.dtype),
            pltpu.SemaphoreType.DMA((count,)),
            pltpu.SemaphoreType.DMA,
        ],
        compiler_params=pltpu.CompilerParams(vmem_limit_bytes=40 * 2**20),
        name="output_rows",
    )(table, *parts, *own, *other, so_far, gate)


def stack_kernel(axis, *refs):
    blocks, out_ref, sems = refs[:-2], refs[-2], refs[-1]
    copies = []
    for i, block in enumerate(blocks):
        cols = block.shape[-1]
        target = out_ref.at[i] if axis == 0 else out_ref.at[:, pl.ds(i * cols, cols)]
        copies.append(pltpu.make_async_copy(block, target, sems.at[i]))
    for copy in copies:
        copy.start()
    for copy in copies:
        copy.wait()


def stack(blocks, axis=0):
    rows, cols = blocks[0].shape
    shape = (len(blocks), rows, cols) if axis == 0 else (rows, len(blocks) * cols)
    return pl.pallas_call(
        functools.partial(stack_kernel, axis),
        in_specs=[pl.BlockSpec(memory_space=pl.ANY)] * len(blocks),
        out_specs=pl.BlockSpec(memory_space=pltpu.VMEM),
        out_shape=jax.ShapeDtypeStruct(shape, blocks[0].dtype),
        scratch_shapes=[pltpu.SemaphoreType.DMA((len(blocks),))],
        name="stack",
    )(*blocks)


def places():
    rows = np.zeros((128, 48), np.int32)
    for tile in range(16):
        for hid in range(8):
            x, yl, yh, z, c = hid // 2, hid % 2, tile // 8, tile // 2 % 4, tile % 2
            row = rows[tile * 8 + hid]
            row[:8] = [(x + s) % 4 * 2 + (yl ^ k) for k in range(2) for s in (0, -way(c), way(c), 2)]
            row[16] = c
            for first, w in ((8, way(c)), (24, -way(c)), (32, way(c)), (40, -way(c))):
                pairs = [(yh ^ k) * 4 + (z + s) % 4 for k in range(2) for s in (0, -w, w, 2)]
                pairs = [pairs[i] for i in (0, 1, 2, 4, 5, 6, 3, 7)]
                if first >= 32:
                    pairs = [rows_held(hid, pair) for pair in pairs]
                row[first : first + 8] = [pairs.index(hid_of) for hid_of in row[:8]]
    return rows


def body(
    residual_in, w_query, w_key, w_value, w_output, shift_mod, scale_mod, gate_mod, neighbours
):
    tok_rows, feat_cols = residual_in.shape
    tile_id, hid_id = lax.axis_index("tile"), lax.axis_index("hid")
    table = lax.dynamic_index_in_dim(jnp.asarray(places()), tile_id * 8 + hid_id, 0, keepdims=False)

    listed = (neighbours >= 0).reshape(PER_LAYER, 3, 3, 3)
    grid = np.arange(PER_LAYER)
    row_step = grid[None, :] // PER_ROW - grid[:, None] // PER_ROW
    col_step = grid[None, :] % PER_ROW - grid[:, None] % PER_ROW
    bias = jnp.full((PER_LAYER, 3, PER_LAYER), -1e30, F32)
    for b in range(-1, 2):
        for e in range(-1, 2):
            here = jnp.asarray((row_step == b) & (col_step == e))[:, None, :]
            bias = jnp.where(here & listed[:, :, b + 1, e + 1][:, :, None], 0.0, bias)
    bias = jnp.repeat(bias.reshape(PER_LAYER, 3 * PER_LAYER), TILE, axis=1)

    gate = lax.dynamic_slice_in_dim(gate_mod, hid_id * feat_cols, feat_cols)[None]

    fence = lax.optimization_barrier
    weights = stack([w_key, w_value, w_query], axis=1)
    kv_cols = 2 * w_key.shape[1]
    w_cols = weights.shape[1]
    x_a, x_b, w_a, w_b, w_mate, own, weights, bias, table, gate, o_block = fence(
        (
            send(residual_in, X_A),
            send(residual_in, X_B),
            send(weights, Z_A),
            send(weights, Z_B),
            send(weights, Y_HI),
            residual_in,
            weights,
            bias,
            table,
            gate,
            w_output,
        )
    )

    far, mate, w_mate_a, w_mate_b, o_block, x_a, x_b, w_a, w_b, own, w_mate, weights = fence(
        (
            send(own, X_2),
            send(own, Y_LO),
            send(w_mate, Z_A),
            send(w_mate, Z_B),
            send(o_block, SWAP_1),
            x_a,
            x_b,
            w_a,
            w_b,
            own,
            w_mate,
            weights,
        )
    )

    mate_a, mate_b, mate_far, w_far, w_mate_far, early, o_block = fence(
        (
            send(mate, X_A),
            send(mate, X_B),
            send(far, Y_LO),
            send(w_a, Z_A),
            send(w_mate_b, Z_B),
            stack([weights, w_a, w_b, w_mate, w_mate_a, w_mate_b]),
            o_block,
        )
    )

    mine = [early, w_far, w_mate_far]
    x_other, first = modulate_project(
        [own, x_a, x_b, far, mate, mate_a, mate_b, mate_far],
        mine,
        table,
        scale_mod.reshape(8, 1, feat_cols),
        shift_mod.reshape(8, 1, feat_cols),
    )
    first, x_other, o_block, *theirs = fence(
        (first, x_other, send(o_block, SWAP_2), *[send(part, CORE) for part in mine])
    )

    key_value = project(x_other, theirs, table, 0, kv_cols, first)
    key_value, o_block, o_a, o_b, o_mate, first, x_other, *theirs = fence(
        (
            key_value,
            o_block,
            send(o_block, Z_A),
            send(o_block, Z_B),
            send(o_block, Y_HI),
            first,
            x_other,
            *theirs,
        )
    )

    queries = project(x_other, theirs, table, kv_cols, w_cols - kv_cols, first)
    before, later, queries, key_value, o_block, o_a, o_b, o_mate = fence(
        (
            send(key_value, NEXT),
            send(key_value, PREV),
            queries,
            key_value,
            o_block,
            o_a,
            o_b,
            o_mate,
        )
    )

    pieces = attend(queries, before, key_value, later, bias)
    o_early = [o_block, o_a, o_b, o_mate]
    pieces, *both = fence((pieces, *o_early, *[send(part, CORE) for part in o_early]))
    o_early, o_early_other = both[:4], both[4:]

    o_mate_a = send(o_early[3], Z_A)
    o_mate_b = send(o_early[3], Z_B)
    p_a, p_b, p_far, p_mate, pieces, *o_late = fence(
        (
            send(pieces, X_A),
            send(pieces, X_B),
            send(pieces, X_2),
            send(pieces, Y_LO),
            pieces,
            o_mate_a,
            o_mate_b,
            send(o_early[1], Z_A),
            send(o_mate_b, Z_B),
        )
    )
    o_mine = [*o_early, *o_late]
    o_theirs = [*o_early_other, *[send(part, CORE) for part in o_late]]
    p_mate_a = send(p_mate, X_A)
    p_mate_b = send(p_mate, X_B)
    p_mate_far = send(p_far, Y_LO)
    near = [pieces, p_a, p_b, p_far, p_mate]
    near = output_rows(near, 0, o_mine, o_theirs, table, residual_in, gate, F32)
    ends = [p_mate_a, p_mate_b, p_mate_far]
    return output_rows(ends, 5, o_mine, o_theirs, table, near, gate, BF16)


def solution(mesh):
    placed = (
        P("tile", "hid"),
        P("tile", "hid"),
        P("tile", "hid"),
        P("tile", "hid"),
        P("hid", "tile"),
        P(),
        P(),
        P(),
        P("tile", None),
    )
    return jax.shard_map(
        body, mesh=mesh, in_specs=placed, out_specs=P("tile", "hid"), check_vma=False
    )
```

```python
import functools

import jax
import jax.numpy as jnp
import numpy as np
from jax import lax
from jax.experimental import pallas as pl
from jax.experimental.pallas import tpu as pltpu
from jax.sharding import PartitionSpec as P

HD = 128
TILE = 32
PER_ROW = 4
PER_LAYER = 16
LAYER = PER_LAYER * TILE
AXES = ("tile", "hid")
F32 = jnp.float32
BF16 = jnp.bfloat16


def route(move):
    pairs = []
    for x in range(4):
        for yl in range(2):
            for yh in range(2):
                for z in range(4):
                    for c in range(2):
                        a, b, d, e, f = move(x, yl, yh, z, c)
                        source = (yh * 8 + z * 2 + c) * 8 + x * 2 + yl
                        target = (d * 8 + e % 4 * 2 + f) * 8 + a % 4 * 2 + b
                        pairs.append((source, target))
    return pairs


def way(c):
    return 1 - 2 * c


X_A = route(lambda x, yl, yh, z, c: (x + way(c), yl, yh, z, c))
X_B = route(lambda x, yl, yh, z, c: (x - way(c), yl, yh, z, c))
X_1 = route(lambda x, yl, yh, z, c: (x ^ 1, yl, yh, z, c))
X_2 = route(lambda x, yl, yh, z, c: (x + 2, yl, yh, z, c))
Z_A = route(lambda x, yl, yh, z, c: (x, yl, yh, z + way(c), c))
Z_2 = route(lambda x, yl, yh, z, c: (x, yl, yh, z + 2, c))
Z_B = route(lambda x, yl, yh, z, c: (x, yl, yh, z - way(c), c))
Y_LO = route(lambda x, yl, yh, z, c: (x, 1 - yl, yh, z, c))
Y_HI = route(lambda x, yl, yh, z, c: (x, yl, 1 - yh, z, c))
CORE = route(lambda x, yl, yh, z, c: (x, yl, yh, z, 1 - c))
SWAP_1 = route(lambda x, yl, yh, z, c: (x, yl, yh ^ x // 2, z + 2 * (x % 2) + yl, c))


def second_move(x, yl, yh, z, c):
    from_z = (z - 2 * (x % 2) - yl) % 4
    return 2 * (yh ^ x // 2) + from_z // 2, from_z % 2, yh, z, c


SWAP_2 = route(second_move)


def rows_held(hid, pair):
    return (pair // 4 ^ hid // 4) * 4 + (pair - hid) % 4


NEXT = [(t * 8 + h, t * 8 + 8 + h) for t in range(15) for h in range(8)]
PREV = [(t * 8 + 8 + h, t * 8 + h) for t in range(15) for h in range(8)]


def send(array, pairs):
    return lax.ppermute(array, AXES, pairs)


def after(array, *others):
    return lax.optimization_barrier((array, *others))[0]


VMEM_BYTES = 60 * 2**20


def place_copies(place, parts, target, sem):
    first = 0
    for part in parts:
        count = part.shape[0] if len(part.shape) == 3 else 1
        source = part.at[jnp.clip(place - first, 0, count - 1)] if len(part.shape) == 3 else part
        here = (place >= first) & (place < first + count)
        yield here, pltpu.make_async_copy(source, target, sem)
        first += count


def start_block(place, parts, target, sem):
    for here, copy in place_copies(place, parts, target, sem):

        @pl.when(here)
        def _():
            copy.start()


def modulate_project_kernel(table, *refs):
    blocks, parts, refs = refs[:8], refs[8:11], refs[11:]
    gain_ref, move_ref, other_out, out_ref, raw, own, other, w_all, x_sems, w_sems, out_sem = refs
    rows, depth = blocks[0].shape
    half = depth // 2
    for i in range(8):
        pltpu.make_async_copy(blocks[i], raw.at[i], x_sems.at[i]).start()

    def fold(value):
        return sum(value[:, lane : lane + 128] for lane in range(0, depth, 128))

    total = jnp.zeros((rows, 128), F32)
    for i in range(8):
        pltpu.make_async_copy(blocks[i], raw.at[i], x_sems.at[i]).wait()
        total += fold(raw[i].astype(F32))
    for i in range(8):
        start_block(table[8 + i], parts, w_all.at[pl.ds(i * half, half), :], w_sems.at[i])
    centre = jnp.sum(total, axis=1, keepdims=True) / (8 * depth)
    spread = jnp.zeros((rows, 128), F32)
    for i in range(8):
        spread += fold(jnp.square(raw[i].astype(F32) - centre))
    scale = lax.rsqrt(jnp.sum(spread, axis=1, keepdims=True) / (8 * depth) + 1e-06)

    def modulate(low_ref, high_ref):
        for i in range(8):
            value = (raw[i].astype(F32) - centre) * scale
            value = (value * (1.0 + gain_ref[table[i]]) + move_ref[table[i]]).astype(BF16)
            low_ref[:, i * half : (i + 1) * half] = value[:, :half]
            high_ref[:, i * half : (i + 1) * half] = value[:, half:]

    @pl.when(table[16] == 0)
    def _():
        modulate(own, other)

    @pl.when(table[16] == 1)
    def _():
        modulate(other, own)

    copy = pltpu.make_async_copy(other, other_out, out_sem)
    copy.start()
    for i in range(8):
        target = w_all.at[pl.ds(i * half, half), :]
        pltpu.make_async_copy(parts[0].at[0], target, w_sems.at[i]).wait()
    out_ref[...] = jnp.dot(own[...], w_all[...], preferred_element_type=F32)
    copy.wait()


def modulate_project(blocks, weights, table, gains, moves):
    rows, depth = blocks[0].shape
    cols = weights[0].shape[2]
    half = (rows, 4 * depth)
    vmem = pl.BlockSpec(memory_space=pltpu.VMEM)
    anywhere = pl.BlockSpec(memory_space=pl.ANY)
    return pl.pallas_call(
        modulate_project_kernel,
        in_specs=[pl.BlockSpec(memory_space=pltpu.SMEM)] + [anywhere] * 11 + [vmem] * 2,
        out_specs=[anywhere, vmem],
        out_shape=[jax.ShapeDtypeStruct(half, BF16), jax.ShapeDtypeStruct((rows, cols), F32)],
        scratch_shapes=[
            pltpu.VMEM((8, rows, depth), BF16),
            pltpu.VMEM(half, BF16),
            pltpu.VMEM(half, BF16),
            pltpu.VMEM((4 * depth, cols), BF16),
            pltpu.SemaphoreType.DMA((8,)),
            pltpu.SemaphoreType.DMA((8,)),
            pltpu.SemaphoreType.DMA,
        ],
        compiler_params=pltpu.CompilerParams(vmem_limit_bytes=VMEM_BYTES),
        name="modulate_project",
    )(table, *blocks, *weights, gains, moves)


def project_kernel(first_col, table, x_ref, *refs):
    parts, (add_ref, out_ref, x_all, w_all, sum_all, x_sems, w_sems, sum_sem) = refs[:3], refs[3:]
    depth = x_ref.shape[1] // 8
    cols = out_ref.shape[1]
    span = pl.ds(first_col, cols)
    parts = [parts[0].at[:, :, span], parts[1].at[:, span], parts[2].at[:, span]]
    pieces = (0, 2, 5, 8)

    def x_copy(n):
        lo, hi = pieces[n], pieces[n + 1]
        here = pl.ds(lo * depth, (hi - lo) * depth)
        return pltpu.make_async_copy(x_ref.at[:, here], x_all.at[:, here], x_sems.at[n])

    def target(i):
        return w_all.at[pl.ds(i * depth, depth), :]

    def start(n):
        x_copy(n).start()
        for i in range(pieces[n], pieces[n + 1]):
            start_block(table[24 + i], parts, target(i), w_sems.at[i])

    sum_copy = pltpu.make_async_copy(add_ref.at[:, span], sum_all, sum_sem)
    start(0)
    start(1)
    total = None
    for n in range(3):
        x_copy(n).wait()
        for i in range(pieces[n], pieces[n + 1]):
            pltpu.make_async_copy(parts[0].at[0], target(i), w_sems.at[i]).wait()
        if n == 0:
            start(2)
            sum_copy.start()
        here = slice(pieces[n] * depth, pieces[n + 1] * depth)
        prod = jnp.dot(x_all[:, here], w_all[here, :], preferred_element_type=F32)
        total = prod if total is None else total + prod
    sum_copy.wait()
    out_ref[...] = (total + sum_all[...]).astype(BF16)


def project(x, weights, table, first_col, cols, add):
    rows, width = x.shape
    return pl.pallas_call(
        functools.partial(project_kernel, first_col),
        in_specs=[pl.BlockSpec(memory_space=pltpu.SMEM)] + [pl.BlockSpec(memory_space=pl.ANY)] * 5,
        out_specs=pl.BlockSpec(memory_space=pltpu.VMEM),
        out_shape=jax.ShapeDtypeStruct((rows, cols), BF16),
        scratch_shapes=[
            pltpu.VMEM((rows, width), BF16),
            pltpu.VMEM((width, cols), BF16),
            pltpu.VMEM((rows, cols), F32),
            pltpu.SemaphoreType.DMA((3,)),
            pltpu.SemaphoreType.DMA((8,)),
            pltpu.SemaphoreType.DMA,
        ],
        compiler_params=pltpu.CompilerParams(vmem_limit_bytes=(60 if first_col == 0 else 50) * 2**20),
        name="project",
    )(table, x, *weights, add)


def attend_kernel(heads, *refs):
    sources, (out_ref, q_ref, prev_ref, own_ref, next_ref, bias_ref, sems) = refs[:5], refs[5:]
    copies = [
        pltpu.make_async_copy(source, target, sems.at[i])
        for i, (source, target) in enumerate(zip(sources, (q_ref, prev_ref, own_ref, next_ref, bias_ref)))
    ]
    for copy in copies:
        copy.start()
    for copy in copies:
        copy.wait()
    width = heads * HD
    row_len = PER_ROW * TILE
    for head in range(heads):
        cols = slice(head * HD, (head + 1) * HD)
        v_cols = slice(width + head * HD, width + (head + 1) * HD)
        for row in range(PER_LAYER // PER_ROW):
            lo = max(row - 1, 0) * row_len
            hi = min(row + 2, PER_LAYER // PER_ROW) * row_len
            queries = q_ref[row * row_len : (row + 1) * row_len, cols]
            scores = []
            for block, ref in enumerate((prev_ref, own_ref, next_ref)):
                part = lax.dot_general(
                    queries,
                    ref[lo:hi, cols],
                    (((1,), (1,)), ((), ())),
                    preferred_element_type=F32,
                ) * HD ** (-0.5)
                tiles = bias_ref[row * PER_ROW : (row + 1) * PER_ROW, block * LAYER + lo : block * LAYER + hi]
                part = part.reshape(PER_ROW, TILE, hi - lo) + tiles[:, None, :]
                scores.append(part.reshape(row_len, hi - lo))
            peak = functools.reduce(
                jnp.maximum, [jnp.max(part, axis=1, keepdims=True) for part in scores]
            )
            chances = [jnp.exp(part - peak) for part in scores]
            denom = sum(jnp.sum(part, axis=1, keepdims=True) for part in chances)
            total = sum(
                jnp.dot(part.astype(BF16), ref[lo:hi, v_cols], preferred_element_type=F32)
                for part, ref in zip(chances, (prev_ref, own_ref, next_ref))
            )
            out_ref[row * row_len : (row + 1) * row_len, cols] = (total / denom).astype(BF16)


def attend(*arrays):
    queries = arrays[0]
    heads = queries.shape[1] // HD
    return pl.pallas_call(
        functools.partial(attend_kernel, heads),
        in_specs=[pl.BlockSpec(memory_space=pl.ANY)] * 5,
        out_specs=pl.BlockSpec(memory_space=pltpu.VMEM),
        out_shape=jax.ShapeDtypeStruct(queries.shape, BF16),
        scratch_shapes=[pltpu.VMEM(array.shape, array.dtype) for array in arrays]
        + [pltpu.SemaphoreType.DMA((5,))],
        compiler_params=pltpu.CompilerParams(vmem_limit_bytes=40 * 2**20),
        name="attend",
    )(*arrays)


def output_kernel(first, count, table, *refs):
    parts, own, other = refs[:count], refs[count : count + 8], refs[count + 8 : count + 16]
    sum_ref, gate_ref, out_ref, x_all, w_all, sum_all, sems, sum_sem = refs[count + 16 :]
    sum_copy = pltpu.make_async_copy(sum_ref, sum_all, sum_sem)
    sum_copy.start()
    core = table[16]
    depth, half = own[0].shape

    def x_copy(i):
        return pltpu.make_async_copy(parts[i], x_all.at[:, pl.ds(i * depth, depth)], sems.at[i])

    def target(i, place):
        cols = pl.ds(pl.multiple_of(place * half, 128), half)
        return w_all.at[pl.ds(i * depth, depth), cols]

    for i in range(count):
        x_copy(i).start()
        for base, refs_of, place in ((32, own, core), (40, other, 1 - core)):
            start_block(table[base + first + i], refs_of, target(i, place), sems.at[i])

    total = None
    for lo in range(0, count, 2):
        hi = min(lo + 2, count)
        for i in range(lo, hi):
            x_copy(i).wait()
            for place in range(2):
                pltpu.make_async_copy(own[0], target(i, place), sems.at[i]).wait()
        span = slice(lo * depth, hi * depth)
        prod = jnp.dot(x_all[:, span], w_all[span, :], preferred_element_type=F32)
        total = prod if total is None else total + prod
    sum_copy.wait()
    out_ref[...] = (sum_all[...].astype(F32) + gate_ref[...] * total).astype(out_ref.dtype)


def output_rows(parts, first, own, other, table, so_far, gate, dtype):
    count = len(parts)
    rows, depth = parts[0].shape
    cols = 2 * own[0].shape[1]
    vmem = pl.BlockSpec(memory_space=pltpu.VMEM)
    anywhere = pl.BlockSpec(memory_space=pl.ANY)
    return pl.pallas_call(
        functools.partial(output_kernel, first, count),
        in_specs=[pl.BlockSpec(memory_space=pltpu.SMEM)] + [anywhere] * (count + 17) + [vmem],
        out_specs=vmem,
        out_shape=jax.ShapeDtypeStruct((rows, cols), dtype),
        scratch_shapes=[
            pltpu.VMEM((rows, count * depth), BF16),
            pltpu.VMEM((count * depth, cols), BF16),
            pltpu.VMEM((rows, cols), so_far.dtype),
            pltpu.SemaphoreType.DMA((count,)),
            pltpu.SemaphoreType.DMA,
        ],
        compiler_params=pltpu.CompilerParams(vmem_limit_bytes=40 * 2**20),
        name="output_rows",
    )(table, *parts, *own, *other, so_far, gate)


def stack_kernel(axis, *refs):
    blocks, out_ref, sems = refs[:-2], refs[-2], refs[-1]
    copies = []
    for i, block in enumerate(blocks):
        cols = block.shape[-1]
        target = out_ref.at[i] if axis == 0 else out_ref.at[:, pl.ds(i * cols, cols)]
        copies.append(pltpu.make_async_copy(block, target, sems.at[i]))
    for copy in copies:
        copy.start()
    for copy in copies:
        copy.wait()


def stack(blocks, axis=0):
    rows, cols = blocks[0].shape
    shape = (len(blocks), rows, cols) if axis == 0 else (rows, len(blocks) * cols)
    return pl.pallas_call(
        functools.partial(stack_kernel, axis),
        in_specs=[pl.BlockSpec(memory_space=pl.ANY)] * len(blocks),
        out_specs=pl.BlockSpec(memory_space=pltpu.VMEM),
        out_shape=jax.ShapeDtypeStruct(shape, blocks[0].dtype),
        scratch_shapes=[pltpu.SemaphoreType.DMA((len(blocks),))],
        name="stack",
    )(*blocks)


def places():
    rows = np.zeros((128, 48), np.int32)
    for tile in range(16):
        for hid in range(8):
            x, yl, yh, z, c = hid // 2, hid % 2, tile // 8, tile // 2 % 4, tile % 2
            row = rows[tile * 8 + hid]
            row[:8] = [(x + s) % 4 * 2 + (yl ^ k) for k in range(2) for s in (0, -way(c), way(c), 2)]
            row[16] = c
            for first, w in ((8, way(c)), (24, -way(c)), (32, way(c)), (40, -way(c))):
                pairs = [(yh ^ k) * 4 + (z + s) % 4 for k in range(2) for s in (0, -w, w, 2)]
                pairs = [pairs[i] for i in (0, 1, 2, 4, 5, 6, 3, 7)]
                if first >= 32:
                    pairs = [rows_held(hid, pair) for pair in pairs]
                row[first : first + 8] = [pairs.index(hid_of) for hid_of in row[:8]]
    return rows


def body(
    residual_in, w_query, w_key, w_value, w_output, shift_mod, scale_mod, gate_mod, neighbours
):
    tok_rows, feat_cols = residual_in.shape
    tile_id, hid_id = lax.axis_index("tile"), lax.axis_index("hid")
    table = lax.dynamic_index_in_dim(jnp.asarray(places()), tile_id * 8 + hid_id, 0, keepdims=False)

    listed = (neighbours >= 0).reshape(PER_LAYER, 3, 3, 3)
    grid = np.arange(PER_LAYER)
    row_step = grid[None, :] // PER_ROW - grid[:, None] // PER_ROW
    col_step = grid[None, :] % PER_ROW - grid[:, None] % PER_ROW
    bias = jnp.full((PER_LAYER, 3, PER_LAYER), -1e30, F32)
    for b in range(-1, 2):
        for e in range(-1, 2):
            here = jnp.asarray((row_step == b) & (col_step == e))[:, None, :]
            bias = jnp.where(here & listed[:, :, b + 1, e + 1][:, :, None], 0.0, bias)
    bias = jnp.repeat(bias.reshape(PER_LAYER, 3 * PER_LAYER), TILE, axis=1)

    gate = lax.dynamic_slice_in_dim(gate_mod, hid_id * feat_cols, feat_cols)[None]

    fence = lax.optimization_barrier
    weights = stack([w_key, w_value, w_query], axis=1)
    kv_cols = 2 * w_key.shape[1]
    w_cols = weights.shape[1]
    x_a, x_b, w_a, w_b, w_mate, own, weights, bias, table, gate, o_block = fence(
        (
            send(residual_in, X_A),
            send(residual_in, X_B),
            send(weights, Z_A),
            send(weights, Z_B),
            send(weights, Y_HI),
            residual_in,
            weights,
            bias,
            table,
            gate,
            w_output,
        )
    )

    far, mate, w_mate_a, w_mate_b, o_block, x_a, x_b, w_a, w_b, own, w_mate, weights = fence(
        (
            send(own, X_2),
            send(own, Y_LO),
            send(w_mate, Z_A),
            send(w_mate, Z_B),
            send(o_block, SWAP_1),
            x_a,
            x_b,
            w_a,
            w_b,
            own,
            w_mate,
            weights,
        )
    )

    mate_a, mate_b, mate_far, w_far, w_mate_far, early, o_block = fence(
        (
            send(mate, X_A),
            send(mate, X_B),
            send(far, Y_LO),
            send(w_a, Z_A),
            send(w_mate_b, Z_B),
            stack([weights, w_a, w_b, w_mate, w_mate_a, w_mate_b]),
            o_block,
        )
    )

    mine = [early, w_far, w_mate_far]
    x_other, first = modulate_project(
        [own, x_a, x_b, far, mate, mate_a, mate_b, mate_far],
        mine,
        table,
        scale_mod.reshape(8, 1, feat_cols),
        shift_mod.reshape(8, 1, feat_cols),
    )
    first, x_other, o_block, *theirs = fence(
        (first, x_other, send(o_block, SWAP_2), *[send(part, CORE) for part in mine])
    )

    key_value = project(x_other, theirs, table, 0, kv_cols, first)
    key_value, o_block, o_a, o_b, o_mate, first, x_other, *theirs = fence(
        (
            key_value,
            o_block,
            send(o_block, Z_A),
            send(o_block, Z_B),
            send(o_block, Y_HI),
            first,
            x_other,
            *theirs,
        )
    )

    queries = project(x_other, theirs, table, kv_cols, w_cols - kv_cols, first)
    before, later, queries, key_value, o_block, o_a, o_b, o_mate = fence(
        (
            send(key_value, NEXT),
            send(key_value, PREV),
            queries,
            key_value,
            o_block,
            o_a,
            o_b,
            o_mate,
        )
    )

    pieces = attend(queries, before, key_value, later, bias)
    o_early = [o_block, o_a, o_b, o_mate]
    pieces, *both = fence((pieces, *o_early, *[send(part, CORE) for part in o_early]))
    o_early, o_early_other = both[:4], both[4:]

    o_mate_a = send(o_early[3], Z_A)
    o_mate_b = send(o_early[3], Z_B)
    p_a, p_b, p_far, p_mate, pieces, *o_late = fence(
        (
            send(pieces, X_A),
            send(pieces, X_B),
            send(pieces, X_2),
            send(pieces, Y_LO),
            pieces,
            o_mate_a,
            o_mate_b,
            send(o_early[1], Z_A),
            send(o_mate_b, Z_B),
        )
    )
    o_mine = [*o_early, *o_late]
    o_theirs = [*o_early_other, *[send(part, CORE) for part in o_late]]
    p_mate_a = send(p_mate, X_A)
    p_mate_b = send(p_mate, X_B)
    p_mate_far = send(p_far, Y_LO)
    near = [pieces, p_a, p_b, p_far, p_mate]
    near = output_rows(near, 0, o_mine, o_theirs, table, residual_in, gate, F32)
    ends = [p_mate_a, p_mate_b, p_mate_far]
    return output_rows(ends, 5, o_mine, o_theirs, table, near, gate, BF16)


def solution(mesh):
    placed = (
        P("tile", "hid"),
        P("tile", "hid"),
        P("tile", "hid"),
        P("tile", "hid"),
        P("hid", "tile"),
        P(),
        P(),
        P(),
        P("tile", None),
    )
    return jax.shard_map(
        body, mesh=mesh, in_specs=placed, out_specs=P("tile", "hid"), check_vma=False
    )
```

```python
import functools

import jax
import jax.numpy as jnp
import numpy as np
from jax import lax
from jax.experimental import pallas as pl
from jax.experimental.pallas import tpu as pltpu
from jax.sharding import PartitionSpec as P

HD = 128
TILE = 32
PER_ROW = 4
PER_LAYER = 16
LAYER = PER_LAYER * TILE
AXES = ("tile", "hid")
F32 = jnp.float32
BF16 = jnp.bfloat16


def route(move):
    pairs = []
    for x in range(4):
        for yl in range(2):
            for yh in range(2):
                for z in range(4):
                    for c in range(2):
                        a, b, d, e, f = move(x, yl, yh, z, c)
                        source = (yh * 8 + z * 2 + c) * 8 + x * 2 + yl
                        target = (d * 8 + e % 4 * 2 + f) * 8 + a % 4 * 2 + b
                        pairs.append((source, target))
    return pairs


def way(c):
    return 1 - 2 * c


X_A = route(lambda x, yl, yh, z, c: (x + way(c), yl, yh, z, c))
X_B = route(lambda x, yl, yh, z, c: (x - way(c), yl, yh, z, c))
X_1 = route(lambda x, yl, yh, z, c: (x ^ 1, yl, yh, z, c))
X_2 = route(lambda x, yl, yh, z, c: (x + 2, yl, yh, z, c))
Z_A = route(lambda x, yl, yh, z, c: (x, yl, yh, z + way(c), c))
Z_2 = route(lambda x, yl, yh, z, c: (x, yl, yh, z + 2, c))
Z_B = route(lambda x, yl, yh, z, c: (x, yl, yh, z - way(c), c))
Y_LO = route(lambda x, yl, yh, z, c: (x, 1 - yl, yh, z, c))
Y_HI = route(lambda x, yl, yh, z, c: (x, yl, 1 - yh, z, c))
CORE = route(lambda x, yl, yh, z, c: (x, yl, yh, z, 1 - c))
SWAP_1 = route(lambda x, yl, yh, z, c: (x, yl, yh ^ x // 2, z + 2 * (x % 2) + yl, c))


def second_move(x, yl, yh, z, c):
    from_z = (z - 2 * (x % 2) - yl) % 4
    return 2 * (yh ^ x // 2) + from_z // 2, from_z % 2, yh, z, c


SWAP_2 = route(second_move)


def rows_held(hid, pair):
    return (pair // 4 ^ hid // 4) * 4 + (pair - hid) % 4


NEXT = [(t * 8 + h, t * 8 + 8 + h) for t in range(15) for h in range(8)]
PREV = [(t * 8 + 8 + h, t * 8 + h) for t in range(15) for h in range(8)]


def send(array, pairs):
    return lax.ppermute(array, AXES, pairs)


def after(array, *others):
    return lax.optimization_barrier((array, *others))[0]


VMEM_BYTES = 60 * 2**20


def place_copies(place, parts, target, sem):
    first = 0
    for part in parts:
        count = part.shape[0] if len(part.shape) == 3 else 1
        source = part.at[jnp.clip(place - first, 0, count - 1)] if len(part.shape) == 3 else part
        here = (place >= first) & (place < first + count)
        yield here, pltpu.make_async_copy(source, target, sem)
        first += count


def start_block(place, parts, target, sem):
    for here, copy in place_copies(place, parts, target, sem):

        @pl.when(here)
        def _():
            copy.start()


def modulate_project_kernel(table, *refs):
    blocks, parts, refs = refs[:8], refs[8:11], refs[11:]
    gain_ref, move_ref, other_out, out_ref, raw, own, other, w_all, x_sems, w_sems, out_sem = refs
    rows, depth = blocks[0].shape
    half = depth // 2
    for i in range(8):
        pltpu.make_async_copy(blocks[i], raw.at[i], x_sems.at[i]).start()

    def fold(value):
        return sum(value[:, lane : lane + 128] for lane in range(0, depth, 128))

    total = jnp.zeros((rows, 128), F32)
    for i in range(8):
        pltpu.make_async_copy(blocks[i], raw.at[i], x_sems.at[i]).wait()
        total += fold(raw[i].astype(F32))
    for i in range(8):
        start_block(table[8 + i], parts, w_all.at[pl.ds(i * half, half), :], w_sems.at[i])
    centre = jnp.sum(total, axis=1, keepdims=True) / (8 * depth)
    spread = jnp.zeros((rows, 128), F32)
    for i in range(8):
        spread += fold(jnp.square(raw[i].astype(F32) - centre))
    scale = lax.rsqrt(jnp.sum(spread, axis=1, keepdims=True) / (8 * depth) + 1e-06)

    def modulate(low_ref, high_ref):
        for i in range(8):
            value = (raw[i].astype(F32) - centre) * scale
            value = (value * (1.0 + gain_ref[table[i]]) + move_ref[table[i]]).astype(BF16)
            low_ref[:, i * half : (i + 1) * half] = value[:, :half]
            high_ref[:, i * half : (i + 1) * half] = value[:, half:]

    @pl.when(table[16] == 0)
    def _():
        modulate(own, other)

    @pl.when(table[16] == 1)
    def _():
        modulate(other, own)

    copy = pltpu.make_async_copy(other, other_out, out_sem)
    copy.start()
    for i in range(8):
        target = w_all.at[pl.ds(i * half, half), :]
        pltpu.make_async_copy(parts[0].at[0], target, w_sems.at[i]).wait()
    out_ref[...] = jnp.dot(own[...], w_all[...], preferred_element_type=F32)
    copy.wait()


def modulate_project(blocks, weights, table, gains, moves):
    rows, depth = blocks[0].shape
    cols = weights[0].shape[2]
    half = (rows, 4 * depth)
    vmem = pl.BlockSpec(memory_space=pltpu.VMEM)
    anywhere = pl.BlockSpec(memory_space=pl.ANY)
    return pl.pallas_call(
        modulate_project_kernel,
        in_specs=[pl.BlockSpec(memory_space=pltpu.SMEM)] + [anywhere] * 11 + [vmem] * 2,
        out_specs=[anywhere, vmem],
        out_shape=[jax.ShapeDtypeStruct(half, BF16), jax.ShapeDtypeStruct((rows, cols), F32)],
        scratch_shapes=[
            pltpu.VMEM((8, rows, depth), BF16),
            pltpu.VMEM(half, BF16),
            pltpu.VMEM(half, BF16),
            pltpu.VMEM((4 * depth, cols), BF16),
            pltpu.SemaphoreType.DMA((8,)),
            pltpu.SemaphoreType.DMA((8,)),
            pltpu.SemaphoreType.DMA,
        ],
        compiler_params=pltpu.CompilerParams(vmem_limit_bytes=VMEM_BYTES),
        name="modulate_project",
    )(table, *blocks, *weights, gains, moves)


def project_kernel(first_col, table, x_ref, *refs):
    parts, (add_ref, out_ref, x_all, w_all, sum_all, x_sems, w_sems, sum_sem) = refs[:3], refs[3:]
    depth = x_ref.shape[1] // 8
    cols = out_ref.shape[1]
    span = pl.ds(first_col, cols)
    parts = [parts[0].at[:, :, span], parts[1].at[:, span], parts[2].at[:, span]]
    pieces = (0, 2, 4, 8)

    def x_copy(n):
        lo, hi = pieces[n], pieces[n + 1]
        here = pl.ds(lo * depth, (hi - lo) * depth)
        return pltpu.make_async_copy(x_ref.at[:, here], x_all.at[:, here], x_sems.at[n])

    def target(i):
        return w_all.at[pl.ds(i * depth, depth), :]

    def start(n):
        x_copy(n).start()
        for i in range(pieces[n], pieces[n + 1]):
            start_block(table[24 + i], parts, target(i), w_sems.at[i])

    sum_copy = pltpu.make_async_copy(add_ref.at[:, span], sum_all, sum_sem)
    start(0)
    start(1)
    total = None
    for n in range(3):
        x_copy(n).wait()
        for i in range(pieces[n], pieces[n + 1]):
            pltpu.make_async_copy(parts[0].at[0], target(i), w_sems.at[i]).wait()
        if n == 0:
            start(2)
            sum_copy.start()
        here = slice(pieces[n] * depth, pieces[n + 1] * depth)
        prod = jnp.dot(x_all[:, here], w_all[here, :], preferred_element_type=F32)
        total = prod if total is None else total + prod
    sum_copy.wait()
    out_ref[...] = (total + sum_all[...]).astype(BF16)


def project(x, weights, table, first_col, cols, add):
    rows, width = x.shape
    return pl.pallas_call(
        functools.partial(project_kernel, first_col),
        in_specs=[pl.BlockSpec(memory_space=pltpu.SMEM)] + [pl.BlockSpec(memory_space=pl.ANY)] * 5,
        out_specs=pl.BlockSpec(memory_space=pltpu.VMEM),
        out_shape=jax.ShapeDtypeStruct((rows, cols), BF16),
        scratch_shapes=[
            pltpu.VMEM((rows, width), BF16),
            pltpu.VMEM((width, cols), BF16),
            pltpu.VMEM((rows, cols), F32),
            pltpu.SemaphoreType.DMA((3,)),
            pltpu.SemaphoreType.DMA((8,)),
            pltpu.SemaphoreType.DMA,
        ],
        compiler_params=pltpu.CompilerParams(vmem_limit_bytes=(60 if first_col == 0 else 50) * 2**20),
        name="project",
    )(table, x, *weights, add)


def attend_kernel(heads, *refs):
    sources, (out_ref, q_ref, prev_ref, own_ref, next_ref, bias_ref, sems) = refs[:5], refs[5:]
    copies = [
        pltpu.make_async_copy(source, target, sems.at[i])
        for i, (source, target) in enumerate(zip(sources, (q_ref, prev_ref, own_ref, next_ref, bias_ref)))
    ]
    for copy in copies:
        copy.start()
    for copy in copies:
        copy.wait()
    width = heads * HD
    row_len = PER_ROW * TILE
    for head in range(heads):
        cols = slice(head * HD, (head + 1) * HD)
        v_cols = slice(width + head * HD, width + (head + 1) * HD)
        for row in range(PER_LAYER // PER_ROW):
            lo = max(row - 1, 0) * row_len
            hi = min(row + 2, PER_LAYER // PER_ROW) * row_len
            queries = q_ref[row * row_len : (row + 1) * row_len, cols]
            scores = []
            for block, ref in enumerate((prev_ref, own_ref, next_ref)):
                part = lax.dot_general(
                    queries,
                    ref[lo:hi, cols],
                    (((1,), (1,)), ((), ())),
                    preferred_element_type=F32,
                ) * HD ** (-0.5)
                tiles = bias_ref[row * PER_ROW : (row + 1) * PER_ROW, block * LAYER + lo : block * LAYER + hi]
                part = part.reshape(PER_ROW, TILE, hi - lo) + tiles[:, None, :]
                scores.append(part.reshape(row_len, hi - lo))
            peak = functools.reduce(
                jnp.maximum, [jnp.max(part, axis=1, keepdims=True) for part in scores]
            )
            chances = [jnp.exp(part - peak) for part in scores]
            denom = sum(jnp.sum(part, axis=1, keepdims=True) for part in chances)
            total = sum(
                jnp.dot(part.astype(BF16), ref[lo:hi, v_cols], preferred_element_type=F32)
                for part, ref in zip(chances, (prev_ref, own_ref, next_ref))
            )
            out_ref[row * row_len : (row + 1) * row_len, cols] = (total / denom).astype(BF16)


def attend(*arrays):
    queries = arrays[0]
    heads = queries.shape[1] // HD
    return pl.pallas_call(
        functools.partial(attend_kernel, heads),
        in_specs=[pl.BlockSpec(memory_space=pl.ANY)] * 5,
        out_specs=pl.BlockSpec(memory_space=pltpu.VMEM),
        out_shape=jax.ShapeDtypeStruct(queries.shape, BF16),
        scratch_shapes=[pltpu.VMEM(array.shape, array.dtype) for array in arrays]
        + [pltpu.SemaphoreType.DMA((5,))],
        compiler_params=pltpu.CompilerParams(vmem_limit_bytes=40 * 2**20),
        name="attend",
    )(*arrays)


def output_kernel(first, count, table, *refs):
    parts, own, other = refs[:count], refs[count : count + 8], refs[count + 8 : count + 16]
    sum_ref, gate_ref, out_ref, x_all, w_all, sum_all, sems, sum_sem = refs[count + 16 :]
    sum_copy = pltpu.make_async_copy(sum_ref, sum_all, sum_sem)
    sum_copy.start()
    core = table[16]
    depth, half = own[0].shape

    def x_copy(i):
        return pltpu.make_async_copy(parts[i], x_all.at[:, pl.ds(i * depth, depth)], sems.at[i])

    def target(i, place):
        cols = pl.ds(pl.multiple_of(place * half, 128), half)
        return w_all.at[pl.ds(i * depth, depth), cols]

    for i in range(count):
        x_copy(i).start()
        for base, refs_of, place in ((32, own, core), (40, other, 1 - core)):
            start_block(table[base + first + i], refs_of, target(i, place), sems.at[i])

    total = None
    for lo in range(0, count, 2):
        hi = min(lo + 2, count)
        for i in range(lo, hi):
            x_copy(i).wait()
            for place in range(2):
                pltpu.make_async_copy(own[0], target(i, place), sems.at[i]).wait()
        span = slice(lo * depth, hi * depth)
        prod = jnp.dot(x_all[:, span], w_all[span, :], preferred_element_type=F32)
        total = prod if total is None else total + prod
    sum_copy.wait()
    out_ref[...] = (sum_all[...].astype(F32) + gate_ref[...] * total).astype(out_ref.dtype)


def output_rows(parts, first, own, other, table, so_far, gate, dtype):
    count = len(parts)
    rows, depth = parts[0].shape
    cols = 2 * own[0].shape[1]
    vmem = pl.BlockSpec(memory_space=pltpu.VMEM)
    anywhere = pl.BlockSpec(memory_space=pl.ANY)
    return pl.pallas_call(
        functools.partial(output_kernel, first, count),
        in_specs=[pl.BlockSpec(memory_space=pltpu.SMEM)] + [anywhere] * (count + 17) + [vmem],
        out_specs=vmem,
        out_shape=jax.ShapeDtypeStruct((rows, cols), dtype),
        scratch_shapes=[
            pltpu.VMEM((rows, count * depth), BF16),
            pltpu.VMEM((count * depth, cols), BF16),
            pltpu.VMEM((rows, cols), so_far.dtype),
            pltpu.SemaphoreType.DMA((count,)),
            pltpu.SemaphoreType.DMA,
        ],
        compiler_params=pltpu.CompilerParams(vmem_limit_bytes=40 * 2**20),
        name="output_rows",
    )(table, *parts, *own, *other, so_far, gate)


def stack_kernel(axis, *refs):
    blocks, out_ref, sems = refs[:-2], refs[-2], refs[-1]
    copies = []
    for i, block in enumerate(blocks):
        cols = block.shape[-1]
        target = out_ref.at[i] if axis == 0 else out_ref.at[:, pl.ds(i * cols, cols)]
        copies.append(pltpu.make_async_copy(block, target, sems.at[i]))
    for copy in copies:
        copy.start()
    for copy in copies:
        copy.wait()


def stack(blocks, axis=0):
    rows, cols = blocks[0].shape
    shape = (len(blocks), rows, cols) if axis == 0 else (rows, len(blocks) * cols)
    return pl.pallas_call(
        functools.partial(stack_kernel, axis),
        in_specs=[pl.BlockSpec(memory_space=pl.ANY)] * len(blocks),
        out_specs=pl.BlockSpec(memory_space=pltpu.VMEM),
        out_shape=jax.ShapeDtypeStruct(shape, blocks[0].dtype),
        scratch_shapes=[pltpu.SemaphoreType.DMA((len(blocks),))],
        name="stack",
    )(*blocks)


def places():
    rows = np.zeros((128, 48), np.int32)
    for tile in range(16):
        for hid in range(8):
            x, yl, yh, z, c = hid // 2, hid % 2, tile // 8, tile // 2 % 4, tile % 2
            row = rows[tile * 8 + hid]
            row[:8] = [(x + s) % 4 * 2 + (yl ^ k) for k in range(2) for s in (0, -way(c), way(c), 2)]
            row[16] = c
            for first, w in ((8, way(c)), (24, -way(c)), (32, way(c)), (40, -way(c))):
                pairs = [(yh ^ k) * 4 + (z + s) % 4 for k in range(2) for s in (0, -w, w, 2)]
                pairs = [pairs[i] for i in (0, 1, 2, 4, 5, 6, 3, 7)]
                if first >= 32:
                    pairs = [rows_held(hid, pair) for pair in pairs]
                row[first : first + 8] = [pairs.index(hid_of) for hid_of in row[:8]]
    return rows


def body(
    residual_in, w_query, w_key, w_value, w_output, shift_mod, scale_mod, gate_mod, neighbours
):
    tok_rows, feat_cols = residual_in.shape
    tile_id, hid_id = lax.axis_index("tile"), lax.axis_index("hid")
    table = lax.dynamic_index_in_dim(jnp.asarray(places()), tile_id * 8 + hid_id, 0, keepdims=False)

    listed = (neighbours >= 0).reshape(PER_LAYER, 3, 3, 3)
    grid = np.arange(PER_LAYER)
    row_step = grid[None, :] // PER_ROW - grid[:, None] // PER_ROW
    col_step = grid[None, :] % PER_ROW - grid[:, None] % PER_ROW
    bias = jnp.full((PER_LAYER, 3, PER_LAYER), -1e30, F32)
    for b in range(-1, 2):
        for e in range(-1, 2):
            here = jnp.asarray((row_step == b) & (col_step == e))[:, None, :]
            bias = jnp.where(here & listed[:, :, b + 1, e + 1][:, :, None], 0.0, bias)
    bias = jnp.repeat(bias.reshape(PER_LAYER, 3 * PER_LAYER), TILE, axis=1)

    gate = lax.dynamic_slice_in_dim(gate_mod, hid_id * feat_cols, feat_cols)[None]

    fence = lax.optimization_barrier
    weights = stack([w_key, w_value, w_query], axis=1)
    kv_cols = 2 * w_key.shape[1]
    w_cols = weights.shape[1]
    x_a, x_b, w_a, w_b, w_mate, own, weights, bias, table, gate, o_block = fence(
        (
            send(residual_in, X_A),
            send(residual_in, X_B),
            send(weights, Z_A),
            send(weights, Z_B),
            send(weights, Y_HI),
            residual_in,
            weights,
            bias,
            table,
            gate,
            w_output,
        )
    )

    far, mate, w_mate_a, w_mate_b, o_block, x_a, x_b, w_a, w_b, own, w_mate, weights = fence(
        (
            send(own, X_2),
            send(own, Y_LO),
            send(w_mate, Z_A),
            send(w_mate, Z_B),
            send(o_block, SWAP_1),
            x_a,
            x_b,
            w_a,
            w_b,
            own,
            w_mate,
            weights,
        )
    )

    mate_a, mate_b, mate_far, w_far, w_mate_far, early, o_block = fence(
        (
            send(mate, X_A),
            send(mate, X_B),
            send(far, Y_LO),
            send(w_a, Z_A),
            send(w_mate_b, Z_B),
            stack([weights, w_a, w_b, w_mate, w_mate_a, w_mate_b]),
            o_block,
        )
    )

    mine = [early, w_far, w_mate_far]
    x_other, first = modulate_project(
        [own, x_a, x_b, far, mate, mate_a, mate_b, mate_far],
        mine,
        table,
        scale_mod.reshape(8, 1, feat_cols),
        shift_mod.reshape(8, 1, feat_cols),
    )
    first, x_other, o_block, *theirs = fence(
        (first, x_other, send(o_block, SWAP_2), *[send(part, CORE) for part in mine])
    )

    key_value = project(x_other, theirs, table, 0, kv_cols, first)
    key_value, o_block, o_a, o_b, o_mate, first, x_other, *theirs = fence(
        (
            key_value,
            o_block,
            send(o_block, Z_A),
            send(o_block, Z_B),
            send(o_block, Y_HI),
            first,
            x_other,
            *theirs,
        )
    )

    queries = project(x_other, theirs, table, kv_cols, w_cols - kv_cols, first)
    before, later, queries, key_value, o_block, o_a, o_b, o_mate = fence(
        (
            send(key_value, NEXT),
            send(key_value, PREV),
            queries,
            key_value,
            o_block,
            o_a,
            o_b,
            o_mate,
        )
    )

    pieces = attend(queries, before, key_value, later, bias)
    o_early = [o_block, o_a, o_b, o_mate]
    pieces, *both = fence((pieces, *o_early, *[send(part, CORE) for part in o_early]))
    o_early, o_early_other = both[:4], both[4:]

    o_mate_a = send(o_early[3], Z_A)
    o_mate_b = send(o_early[3], Z_B)
    p_a, p_b, p_far, p_mate, pieces, *o_late = fence(
        (
            send(pieces, X_A),
            send(pieces, X_B),
            send(pieces, X_2),
            send(pieces, Y_LO),
            pieces,
            o_mate_a,
            o_mate_b,
            send(o_early[1], Z_A),
            send(o_mate_b, Z_B),
        )
    )
    o_mine = [*o_early, *o_late]
    o_theirs = [*o_early_other, *[send(part, CORE) for part in o_late]]
    p_mate_a = send(p_mate, X_A)
    p_mate_b = send(p_mate, X_B)
    p_mate_far = send(p_far, Y_LO)
    near = [pieces, p_a, p_b, p_far, p_mate]
    near = output_rows(near, 0, o_mine, o_theirs, table, residual_in, gate, F32)
    ends = [p_mate_a, p_mate_b, p_mate_far]
    return output_rows(ends, 5, o_mine, o_theirs, table, near, gate, BF16)


def solution(mesh):
    placed = (
        P("tile", "hid"),
        P("tile", "hid"),
        P("tile", "hid"),
        P("tile", "hid"),
        P("hid", "tile"),
        P(),
        P(),
        P(),
        P("tile", None),
    )
    return jax.shard_map(
        body, mesh=mesh, in_specs=placed, out_specs=P("tile", "hid"), check_vma=False
    )
```
